32 devices in a mesh: ri: 4 (over x, core), row: 2 (over y), col: 4 (over z).
Axes of the slice: x: 2, y: 2, z: 4, core: 2. Of those that a mesh axis runs over, the one named last changes fastest.
Arguments:
- three_centre: bfloat16 [32, 256, 2048], P('ri', 'row', 'col'), may hold values from -1 to 1
- density_band: bfloat16 [2048, 5, 128], P('col'), may hold values from -0.25 to 0.25
- band_mask: int32 [16, 5], P('col'), may hold values 0 or 1
Outputs:
- exchange: float32 [256, 256], P('col', 'row')
The draws below stay inside these ranges and needn't reach their ends.
All inputs are finite; a program needn't handle non-finite values. No bound on the sum of `band_mask` on one device may be relied on, other than what follows from the above.
Results may differ from the reference program's by a relative error of at most 0.0029.
Values may be sent and summed in bfloat16 or wider, within the bound.
No kernel may reach another device: no remote copies, remote signals or barrier semaphores. Data moves between devices by JAX's collectives and lax.ppermute only.
A program may use at most 64 MiB of HBM per device.

```python
import jax
import jax.numpy as jnp
from jax import lax

RI_DEV = 8
COL_ORB = 128
BLK_DEV = 4
BAND = 5
RI_FUNCS = 32
ROWS = 256
COL_BLOCKS = 16
COLS = 2048
N_RI = 4
N_COL = 4


def plant(values, stream_key, low, high):
    dims = values.shape
    spot = [jax.random.randint(jax.random.fold_in(stream_key, axis), (), 0, dims[axis]) for axis in range(len(dims))]
    values = values.at[tuple(spot)].set(low)
    longest = dims.index(max(dims))
    spot[longest] = (spot[longest] + 1) % dims[longest]
    return values.at[tuple(spot)].set(high)


def block_levels(rng, dims, shards, smallest, high):
    def one(position, parts):
        steps = jax.random.uniform(jax.random.fold_in(jax.random.fold_in(rng, 6), position), (parts,), jnp.float32, smallest / len(shards), high / len(shards))
        return jnp.repeat(jnp.exp(steps), dims[position] // parts).reshape((-1,) + (1,) * (len(dims) - position - 1))

    factor_of = one(*shards[0])
    for cut in shards[1:]:
        factor_of = factor_of * one(*cut)
    return factor_of


def normal_values(rng, extent, deviation, reach, pieces=(), dtype=jnp.bfloat16):
    factor_of = block_levels(rng, extent, pieces, -0.22, 0.18) if pieces else 1.0
    drawn = jax.random.normal(rng, extent, jnp.float32) * deviation * factor_of
    return jnp.minimum(jnp.maximum(drawn, -reach), reach).astype(dtype)


def setup_inputs(seed: int = 0) -> dict:
    streams_of = jax.random.split(jax.random.key(seed), 4)
    three_centre = normal_values(streams_of[0], (RI_FUNCS, ROWS, COLS), ((RI_DEV * N_RI * COL_ORB * BLK_DEV * N_COL) ** -0.25), 1.0, ((0, 4), (1, 2), (2, 4)))
    density_band = normal_values(streams_of[1], (COLS, BAND, COL_ORB), (BAND * COL_ORB) ** -0.5, 0.25, ((0, 4),))
    band_mask = plant((jax.random.randint(streams_of[2], (COL_BLOCKS, BAND), 0, 4) < 3).astype(jnp.int32), jax.random.fold_in(streams_of[2], 1), 0, 1)
    return dict(three_centre=three_centre, density_band=density_band, band_mask=band_mask)


def reference(three_centre, density_band, band_mask):
    col_orb = density_band.shape[2]
    band_count = density_band.shape[1]
    centre = band_count // 2
    blocks = band_mask.shape[0]
    rows = three_centre.shape[1]
    weights = jnp.repeat(band_mask.astype(jnp.float32), col_orb, axis=0)[:, :, None]
    density = (density_band.astype(jnp.float32) * weights).astype(jnp.bfloat16)
    density_blocks = density.astype(jnp.float32).reshape(blocks, col_orb, band_count, col_orb)

    def one_function(total, tensor_row):
        tensor_full = tensor_row.astype(jnp.float32)
        tensor_blocks = tensor_full.reshape(rows, blocks, col_orb)
        mixed = jnp.zeros((rows, blocks, col_orb), jnp.float32)
        for column in range(band_count):
            part = jnp.einsum("mbl,bls->mbs", tensor_blocks, density_blocks[:, :, column, :])
            mixed = mixed + jnp.roll(part, column - centre, axis=1)
        mixed_low = lax.optimization_barrier(mixed.reshape(rows, blocks * col_orb).astype(jnp.bfloat16))
        mixed_back = mixed_low.astype(jnp.float32)
        return total + jnp.dot(tensor_full, mixed_back.T, preferred_element_type=jnp.float32), None

    start = jnp.zeros((rows, rows), jnp.float32)
    result, unused = lax.scan(one_function, start, three_centre)
    return result
```

```python
import functools

import jax
import jax.numpy as jnp
from jax import lax
from jax.experimental import pallas as pl
from jax.experimental.pallas import tpu as pltpu
from jax.sharding import PartitionSpec as P

AXES = ("ri", "row", "col")
F32 = jnp.float32
BF16 = jnp.bfloat16


def move(value, sizes, target):
    pairs = []
    for i in range(sizes[0]):
        for j in range(sizes[1]):
            for k in range(sizes[2]):
                to = target(i, j, k)
                if to is not None:
                    pairs.append(((i * sizes[1] + j) * sizes[2] + k, (to[0] * sizes[1] + to[1]) * sizes[2] + to[2]))
    return lax.ppermute(value, AXES, pairs)


def owned(rows, cols):
    offsets = [(a, b) for a in range(rows) for b in range(cols)]
    half = len(offsets) // 2
    first = offsets[1:half] + offsets[:1]
    return first, offsets[half:]


def window_dot(parts, lo, hi):
    return jnp.concatenate([part[:, lo:hi] for part in parts], axis=0)


def exchange_kernel(plan, sizes, centre, edge_ref, *refs):
    n_row = sizes[1]
    own_ref = refs[0]
    others = refs[1:n_row]
    halo_ref = refs[n_row]
    halo_others = refs[n_row + 1 : 2 * n_row]
    dens_ref, mask_ref, keep_ref, give_ref, band_ref, kx_ref = refs[2 * n_row :]
    groups = (own_ref,) + others
    halos = (halo_ref,) + halo_others
    chunk, rows, cols = own_ref.shape
    band_count, unused, orb = dens_ref.shape
    blocks = cols // orb
    wide = centre * orb

    band_ref[...] = jnp.zeros_like(band_ref)
    for l in range(blocks):
        for c in range(band_count):
            s = l + c - centre
            if -centre <= s < blocks:
                block = dens_ref[c, l * orb : (l + 1) * orb, :]
                kept = mask_ref[l, c] != 0
                band_ref[(l + centre) * orb : (l + centre + 1) * orb, (s + centre) * orb : (s + centre + 1) * orb] = (
                    jnp.where(kept, block, jnp.zeros_like(block))
                )
    band_ref[:wide, wide : 2 * wide] = edge_ref[...]

    def body(p, total):
        window = jnp.concatenate(
            [jnp.concatenate([halo[p] for halo in halos], axis=0), jnp.concatenate([group[p] for group in groups], axis=0)],
            axis=1,
        )
        parts = []
        for lo in range(0, cols + wide, wide):
            l_lo = wide if lo == 0 else max(0, lo - 2 * wide + wide)
            l_hi = min(cols + wide, lo + 2 * wide)
            parts.append(
                jnp.dot(
                    window[:, l_lo:l_hi],
                    band_ref[l_lo:l_hi, lo : lo + wide],
                    preferred_element_type=F32,
                ).astype(BF16)
            )
        mixed = jnp.concatenate(parts, axis=1)
        return total + lax.dot_general(window, mixed, (((1,), (1,)), ((), ())), preferred_element_type=F32)

    total = jnp.zeros((n_row * rows, n_row * rows), F32)
    for p in range(chunk):
        total = body(p, total)
    for d in range(n_row):
        kx_ref[d] = total[:, d * rows : (d + 1) * rows]

    core = lax.rem(lax.axis_index("ri"), 2)
    row = lax.axis_index("row")
    col = lax.axis_index("col")
    out_rows = n_row * rows // sizes[2]
    per_group = rows // out_rows
    for ref, side in ((keep_ref, core), (give_ref, 1 - core)):
        for k, (zero, one) in enumerate(zip(*plan)):
            dr = jnp.where(side == 0, zero[0], one[0])
            to_col = col ^ jnp.where(side == 0, zero[1], one[1])
            start = ((to_col // per_group) ^ row) * rows + (to_col % per_group) * out_rows
            ref[k] = kx_ref[dr, pl.ds(pl.multiple_of(start, out_rows), out_rows), :]


def per_device(sizes, three_centre, density_band, band_mask):
    n_ri, n_row, n_col = sizes
    funcs, rows, cols = three_centre.shape
    band_count, orb = density_band.shape[1:]
    centre = band_count // 2
    wide = centre * orb
    chunk = funcs // n_row
    row = lax.axis_index("row")
    core = lax.rem(lax.axis_index("ri"), 2)
    plan = owned(n_row, n_col)

    chunks = three_centre.reshape(n_row, chunk, rows, cols)
    mine = lax.dynamic_index_in_dim(chunks, row, 0, keepdims=False)
    theirs = [lax.dynamic_index_in_dim(chunks, row ^ d, 0, keepdims=False) for d in range(1, n_row)]
    density = jnp.transpose(density_band, (1, 0, 2))

    last = cols - wide
    lines = []
    for j in range(centre):
        line = []
        for s in range(centre):
            c = s - j + 2 * centre
            if c < band_count:
                block = density[c, last + j * orb : last + (j + 1) * orb, :]
                line.append(jnp.where(band_mask[cols // orb - centre + j, c] != 0, block, jnp.zeros_like(block)))
            else:
                line.append(jnp.zeros((orb, orb), BF16))
        lines.append(jnp.concatenate(line, axis=1))
    edge = jnp.concatenate(lines, axis=0)

    others = [
        move(theirs[d - 1], sizes, lambda i, j, k, d=d: (i, j ^ d, k)) for d in range(1, n_row)
    ]
    halo_others = [
        move(theirs[d - 1][:, :, last:], sizes, lambda i, j, k, d=d: (i, j ^ d, (k + 1) % n_col))
        for d in range(1, n_row)
    ]
    packed = jnp.concatenate([mine[:, :, last:].reshape(chunk * rows, wide), edge], axis=0)
    packed = move(packed, sizes, lambda i, j, k: (i, j, (k + 1) % n_col))
    halo = packed[: chunk * rows].reshape(chunk, rows, wide)
    edge = packed[chunk * rows :]

    half = n_row * n_col // 2
    out_rows = n_row * rows // n_col
    vmem = pl.BlockSpec(memory_space=pltpu.VMEM)
    window = cols + wide
    keep, give = pl.pallas_call(
        functools.partial(exchange_kernel, plan, sizes, centre),
        out_shape=[jax.ShapeDtypeStruct((half, out_rows, rows), F32)] * 2,
        in_specs=[vmem] * (2 * n_row + 2) + [pl.BlockSpec(memory_space=pltpu.SMEM)],
        out_specs=[vmem] * 2,
        scratch_shapes=[
            pltpu.VMEM((window, window), BF16),
            pltpu.VMEM((n_row, n_row * rows, rows), F32),
        ],
        compiler_params=pltpu.CompilerParams(vmem_limit_bytes=32 * 1024 * 1024),
    )(edge, mine, *others, halo, *halo_others, density, band_mask)

    got = move(give, sizes, lambda i, j, k: (i ^ 1, j, k))
    pieces = keep + got
    total = jnp.where(core == 0, pieces[half - 1], 0.0)
    for n, (zero, one) in enumerate(zip(*plan)):
        def target(i, j, k):
            dr, dc = one if i % 2 else zero
            return None if (dr, dc) == (0, 0) else (i, j ^ dr, k ^ dc)

        total = total + move(pieces[n], sizes, target)
    result = total
    for d in range(1, n_ri):
        result = result + move(total, sizes, lambda i, j, k, d=d: (i ^ d, j, k))
    return result


def solution(mesh):
    sizes = tuple(mesh.shape[axis] for axis in AXES)
    placed = (P("ri", "row", "col"), P("col", None, None), P("col", None))
    return jax.shard_map(
        functools.partial(per_device, sizes), mesh=mesh, in_specs=placed, out_specs=P("col", "row"), check_vma=False
    )
```

```python
import functools

import jax
import jax.numpy as jnp
from jax import lax
from jax.experimental import pallas as pl
from jax.experimental.pallas import tpu as pltpu
from jax.sharding import PartitionSpec as P

AXES = ("ri", "row", "col")
F32 = jnp.float32
BF16 = jnp.bfloat16
VMEM = pl.BlockSpec(memory_space=pltpu.VMEM)
SMEM = pl.BlockSpec(memory_space=pltpu.SMEM)
PARAMS = pltpu.CompilerParams(vmem_limit_bytes=32 * 1024 * 1024)


def move(value, sizes, target):
    pairs = []
    for i in range(sizes[0]):
        for j in range(sizes[1]):
            for k in range(sizes[2]):
                to = target(i, j, k)
                if to is not None:
                    pairs.append(((i * sizes[1] + j) * sizes[2] + k, (to[0] * sizes[1] + to[1]) * sizes[2] + to[2]))
    return lax.ppermute(value, AXES, pairs)


def after(value, *earlier):
    return lax.optimization_barrier((value,) + earlier)[0]


def owned(rows, cols):
    offsets = [(a, b) for a in range(rows) for b in range(cols)]
    half = len(offsets) // 2
    first = offsets[1:half] + offsets[:1]
    return first, offsets[half:]


def times(a, b):
    return jnp.dot(a, b, preferred_element_type=F32)


def times_turned(a, b):
    return lax.dot_general(a, b, (((1,), (1,)), ((), ())), preferred_element_type=F32)


def density_kernel(centre, mask_ref, dens_ref, local_ref, back_ref, edge_ref, whole_ref):
    band_count, cols, orb = dens_ref.shape
    blocks = cols // orb
    local_ref[...] = jnp.zeros_like(local_ref)
    back_ref[...] = jnp.zeros_like(back_ref)
    whole_ref[...] = jnp.zeros_like(whole_ref)
    for l in range(blocks):
        for c in range(band_count):
            block = dens_ref[c, l * orb : (l + 1) * orb, :]
            block = jnp.where(mask_ref[l, c] != 0, block, jnp.zeros_like(block))
            s = l + c - centre
            if s < 0:
                back_ref[l * orb : (l + 1) * orb, (s + centre) * orb : (s + centre + 1) * orb] = block
            elif s < blocks:
                local_ref[l * orb : (l + 1) * orb, s * orb : (s + 1) * orb] = block
            else:
                first = l - blocks + centre
                whole_ref[first * orb : (first + 1) * orb, (s - blocks) * orb : (s - blocks + 1) * orb] = block
    half = edge_ref.shape[0]
    core = lax.rem(lax.axis_index("ri"), 2)
    edge_ref[...] = whole_ref[pl.ds(pl.multiple_of(core * half, half), half), :]


def inner_kernel(count, wide, *refs):
    own_ref = refs[0]
    rests = refs[1:count]
    edges = refs[count : 2 * count - 1]
    local_ref, total_ref, open_ref = refs[2 * count - 1 :]
    chunk, rows, cols = own_ref.shape
    total = None
    for p in range(chunk):
        left = jnp.concatenate([own_ref[p, :, : cols - wide]] + [ref[p] for ref in rests], axis=0)
        right = jnp.concatenate([own_ref[p, :, cols - wide :]] + [ref[p] for ref in edges], axis=0)
        held = jnp.concatenate([left, right], axis=1)
        mixed = []
        for lo in range(0, cols, wide):
            l_lo, l_hi = max(0, lo - wide), min(cols, lo + 2 * wide)
            mixed.append(times(held[:, l_lo:l_hi], local_ref[l_lo:l_hi, lo : lo + wide]))
        open_ref[p] = mixed[0]
        closed = jnp.concatenate([part.astype(BF16) for part in mixed[1:]], axis=1)
        part = times_turned(held[:, wide:], closed)
        total = part if total is None else total + part
    total_ref[...] = total


def outer_kernel(count, plan, sizes, *refs):
    own_ref = refs[0]
    rests = refs[1:count]
    halos = refs[count : 2 * count]
    back_ref, mine_ref, partner_ref, inner_ref, open_ref, keep_ref, give_ref, edge_ref, kx_ref = refs[2 * count :]
    chunk, rows, wide = halos[0].shape
    half = mine_ref.shape[0]
    core = lax.rem(lax.axis_index("ri"), 2)
    row = lax.axis_index("row")
    col = lax.axis_index("col")
    edge_ref[pl.ds(pl.multiple_of(core * half, half), half), :] = mine_ref[...]
    edge_ref[pl.ds(pl.multiple_of((1 - core) * half, half), half), :] = partner_ref[...]
    total = inner_ref[...]
    for p in range(chunk):
        near = jnp.concatenate([own_ref[p, :, :wide]] + [ref[p, :, :wide] for ref in rests], axis=0)
        halo = jnp.concatenate([ref[p] for ref in halos], axis=0)
        mixed = (open_ref[p] + times(halo, edge_ref[...])).astype(BF16)
        behind = times(near, back_ref[...]).astype(BF16)
        total = total + times_turned(
            jnp.concatenate([near, halo], axis=1), jnp.concatenate([mixed, behind], axis=1)
        )
    for d in range(count):
        kx_ref[d] = total[:, d * rows : (d + 1) * rows]
    out_rows = count * rows // sizes[2]
    per_group = rows // out_rows
    for ref, side in ((give_ref, 1 - core), (keep_ref, core)):
        for k, (zero, one) in enumerate(zip(*plan)):
            dr = jnp.where(side == 0, zero[0], one[0])
            to_col = col ^ jnp.where(side == 0, zero[1], one[1])
            start = ((to_col // per_group) ^ row) * rows + (to_col % per_group) * out_rows
            ref[k] = kx_ref[dr, pl.ds(pl.multiple_of(start, out_rows), out_rows), :]


def per_device(sizes, three_centre, density_band, band_mask):
    n_ri, n_row, n_col = sizes
    funcs, rows, cols = three_centre.shape
    band_count, orb = density_band.shape[1:]
    centre = band_count // 2
    wide = centre * orb
    last = cols - wide
    chunk = funcs // n_row
    row = lax.axis_index("row")
    core = lax.rem(lax.axis_index("ri"), 2)
    plan = owned(n_row, n_col)

    def forward(i, j, k):
        return i, j, (k + 1) % n_col

    def pick(index, lo, hi):
        cut = lax.dynamic_slice(three_centre, (index * chunk, 0, lo), (chunk, rows, hi - lo))
        return cut

    edges = [move(pick(row ^ d, last, cols), sizes, lambda i, j, k, d=d: (i, j ^ d, k)) for d in range(1, n_row)]
    halos = [move(pick(row, last, cols), sizes, forward)]
    mine = pick(row, 0, cols)

    local, back, edge = pl.pallas_call(
        functools.partial(density_kernel, centre),
        out_shape=[
            jax.ShapeDtypeStruct((cols, cols), BF16),
            jax.ShapeDtypeStruct((wide, wide), BF16),
            jax.ShapeDtypeStruct((wide // 2, wide), BF16),
        ],
        in_specs=[SMEM, VMEM],
        out_specs=[VMEM] * 3,
        scratch_shapes=[pltpu.VMEM((wide, wide), BF16)],
        compiler_params=PARAMS,
        cost_estimate=pl.CostEstimate(flops=10**10, bytes_accessed=1, transcendentals=0),
    )(band_mask, jnp.transpose(density_band, (1, 0, 2)))
    edge = move(edge, sizes, forward)
    partner = move(edge, sizes, lambda i, j, k: (i ^ 1, j, k))

    rests = [
        move(after(pick(row ^ d, 0, last), edges[d - 1]), sizes, lambda i, j, k, d=d: (i, j ^ d, k))
        for d in range(1, n_row)
    ]
    halos += [move(part, sizes, forward) for part in edges]

    whole = n_row * rows
    total, open_part = pl.pallas_call(
        functools.partial(inner_kernel, n_row, wide),
        out_shape=[jax.ShapeDtypeStruct((whole, whole), F32), jax.ShapeDtypeStruct((chunk, whole, wide), F32)],
        in_specs=[VMEM] * (2 * n_row),
        out_specs=[VMEM] * 2,
        compiler_params=PARAMS,
        cost_estimate=pl.CostEstimate(flops=1, bytes_accessed=1, transcendentals=0),
    )(mine, *rests, *edges, local)

    half = n_row * n_col // 2
    out_rows = whole // n_col
    keep, give = pl.pallas_call(
        functools.partial(outer_kernel, n_row, plan, sizes),
        out_shape=[jax.ShapeDtypeStruct((half, out_rows, rows), F32)] * 2,
        in_specs=[VMEM] * (2 * n_row + 5),
        out_specs=[VMEM] * 2,
        scratch_shapes=[pltpu.VMEM((wide, wide), BF16), pltpu.VMEM((n_row, whole, rows), F32)],
        compiler_params=PARAMS,
        cost_estimate=pl.CostEstimate(flops=1, bytes_accessed=1, transcendentals=0),
    )(mine, *rests, *halos, back, edge, partner, total, open_part)

    got = move(give, sizes, lambda i, j, k: (i ^ 1, j, k))
    pieces = keep + got
    total = jnp.where(core == 0, pieces[half - 1], 0.0)
    for n, (zero, one) in enumerate(zip(*plan)):
        def target(i, j, k):
            dr, dc = one if i % 2 else zero
            return None if (dr, dc) == (0, 0) else (i, j ^ dr, k ^ dc)

        total = total + move(pieces[n], sizes, target)
    result = total
    for d in range(2, n_ri, 2):
        result = result + move(total, sizes, lambda i, j, k, d=d: (i ^ d, j, k))
    return result + move(result, sizes, lambda i, j, k: (i ^ 1, j, k))


def solution(mesh):
    sizes = tuple(mesh.shape[axis] for axis in AXES)
    placed = (P("ri", "row", "col"), P("col", None, None), P("col", None))
    return jax.shard_map(
        functools.partial(per_device, sizes), mesh=mesh, in_specs=placed, out_specs=P("col", "row"), check_vma=False
    )
```

```python
import functools

import jax
import jax.numpy as jnp
from jax import lax
from jax.experimental import pallas as pl
from jax.experimental.pallas import tpu as pltpu
from jax.sharding import PartitionSpec as P

AXES = ("ri", "row", "col")
F32 = jnp.float32
BF16 = jnp.bfloat16
VMEM = pl.BlockSpec(memory_space=pltpu.VMEM)
SMEM = pl.BlockSpec(memory_space=pltpu.SMEM)
PARAMS = pltpu.CompilerParams(vmem_limit_bytes=32 * 1024 * 1024)


def move(value, sizes, target):
    pairs = []
    for i in range(sizes[0]):
        for j in range(sizes[1]):
            for k in range(sizes[2]):
                to = target(i, j, k)
                if to is not None:
                    pairs.append(((i * sizes[1] + j) * sizes[2] + k, (to[0] * sizes[1] + to[1]) * sizes[2] + to[2]))
    return lax.ppermute(value, AXES, pairs)


def after(value, *earlier):
    return lax.optimization_barrier((value,) + earlier)[0]


def owned(rows, cols):
    offsets = [(a, b) for a in range(rows) for b in range(cols)]
    half = len(offsets) // 2
    first = offsets[1:half] + offsets[:1]
    return first, offsets[half:]


def times(a, b):
    return jnp.dot(a, b, preferred_element_type=F32)


def times_turned(a, b):
    return lax.dot_general(a, b, (((1,), (1,)), ((), ())), preferred_element_type=F32)


def masked(mask_ref, dens_ref, l, c):
    orb = dens_ref.shape[2]
    block = dens_ref[c, l * orb : (l + 1) * orb, :]
    return jnp.where(mask_ref[l, c] != 0, block, jnp.zeros_like(block))


def beyond(centre):
    return [(l, s) for l in range(centre) for s in range(l + 1)]


def pack_kernel(centre, mask_ref, dens_ref, last_ref, out_ref):
    band_count, cols, orb = dens_ref.shape
    blocks = cols // orb
    chunk, rows, unused = last_ref.shape
    for p in range(chunk):
        for j in range(centre):
            at = (p * centre + j) * rows
            out_ref[at : at + rows, :] = last_ref[p, :, j * orb : (j + 1) * orb]
    at = chunk * centre * rows
    for l, s in beyond(centre):
        out_ref[at : at + orb, :] = masked(mask_ref, dens_ref, blocks - centre + l, s - l + 2 * centre)
        at += orb


def band_kernel(centre, mask_ref, dens_ref, local_ref, back_ref):
    band_count, cols, orb = dens_ref.shape
    blocks = cols // orb
    local_ref[...] = jnp.zeros_like(local_ref)
    back_ref[...] = jnp.zeros_like(back_ref)
    for l in range(blocks):
        for c in range(band_count):
            s = l + c - centre
            if s < 0:
                back_ref[l * orb : (l + 1) * orb, (s + centre) * orb : (s + centre + 1) * orb] = masked(
                    mask_ref, dens_ref, l, c
                )
            elif s < blocks:
                local_ref[l * orb : (l + 1) * orb, s * orb : (s + 1) * orb] = masked(mask_ref, dens_ref, l, c)


def inner_kernel(count, wide, *refs):
    own_ref = refs[0]
    rests = refs[1:count]
    edges = refs[count : 2 * count - 1]
    local_ref, total_ref, open_ref = refs[2 * count - 1 :]
    chunk, rows, cols = own_ref.shape
    total = None
    for p in range(chunk):
        left = jnp.concatenate([own_ref[p, :, : cols - wide]] + [ref[p] for ref in rests], axis=0)
        right = jnp.concatenate([own_ref[p, :, cols - wide :]] + [ref[p] for ref in edges], axis=0)
        held = jnp.concatenate([left, right], axis=1)
        mixed = []
        for lo in range(0, cols, wide):
            l_lo, l_hi = max(0, lo - wide), min(cols, lo + 2 * wide)
            mixed.append(times(held[:, l_lo:l_hi], local_ref[l_lo:l_hi, lo : lo + wide]))
        open_ref[p] = mixed[0]
        closed = jnp.concatenate([part.astype(BF16) for part in mixed[1:]], axis=1)
        part = times_turned(held[:, wide:], closed)
        total = part if total is None else total + part
    total_ref[...] = total


def outer_kernel(count, centre, plan, sizes, *refs):
    own_ref = refs[0]
    rests = refs[1:count]
    packed_ref = refs[count]
    halos = refs[count + 1 : 2 * count]
    back_ref, inner_ref, open_ref, keep_ref, give_ref, edge_ref, kx_ref = refs[2 * count :]
    chunk, rows, unused = own_ref.shape
    orb = packed_ref.shape[1]
    wide = centre * orb
    core = lax.rem(lax.axis_index("ri"), 2)
    row = lax.axis_index("row")
    col = lax.axis_index("col")
    edge_ref[...] = jnp.zeros_like(edge_ref)
    at = chunk * centre * rows
    for l, s in beyond(centre):
        edge_ref[l * orb : (l + 1) * orb, s * orb : (s + 1) * orb] = packed_ref[at : at + orb, :]
        at += orb
    total = inner_ref[...]
    for p in range(chunk):
        near = jnp.concatenate([own_ref[p, :, :wide]] + [ref[p, :, :wide] for ref in rests], axis=0)
        starts = [(p * centre + j) * rows for j in range(centre)]
        first = jnp.concatenate([packed_ref[at : at + rows, :] for at in starts], axis=1)
        halo = jnp.concatenate([first] + [ref[p] for ref in halos], axis=0)
        mixed = (open_ref[p] + times(halo, edge_ref[...])).astype(BF16)
        behind = times(near, back_ref[...]).astype(BF16)
        total = total + times_turned(
            jnp.concatenate([near, halo], axis=1), jnp.concatenate([mixed, behind], axis=1)
        )
    for d in range(count):
        kx_ref[d] = total[:, d * rows : (d + 1) * rows]
    out_rows = count * rows // sizes[2]
    per_group = rows // out_rows
    for ref, side in ((give_ref, 1 - core), (keep_ref, core)):
        for k, (zero, one) in enumerate(zip(*plan)):
            dr = jnp.where(side == 0, zero[0], one[0])
            to_col = col ^ jnp.where(side == 0, zero[1], one[1])
            start = ((to_col // per_group) ^ row) * rows + (to_col % per_group) * out_rows
            ref[k] = kx_ref[dr, pl.ds(pl.multiple_of(start, out_rows), out_rows), :]


def per_device(sizes, three_centre, density_band, band_mask):
    n_ri, n_row, n_col = sizes
    funcs, rows, cols = three_centre.shape
    band_count, orb = density_band.shape[1:]
    centre = band_count // 2
    wide = centre * orb
    last = cols - wide
    chunk = funcs // n_row
    row = lax.axis_index("row")
    core = lax.rem(lax.axis_index("ri"), 2)
    plan = owned(n_row, n_col)

    def forward(i, j, k):
        return i, j, (k + 1) % n_col

    def pick(index, lo, hi):
        cut = lax.dynamic_slice(three_centre, (index * chunk, 0, lo), (chunk, rows, hi - lo))
        return cut

    density = jnp.transpose(density_band, (1, 0, 2))
    edges = [move(pick(row ^ d, last, cols), sizes, lambda i, j, k, d=d: (i, j ^ d, k)) for d in range(1, n_row)]
    packed = pl.pallas_call(
        functools.partial(pack_kernel, centre),
        out_shape=jax.ShapeDtypeStruct((chunk * centre * rows + len(beyond(centre)) * orb, orb), BF16),
        in_specs=[SMEM, VMEM, VMEM],
        out_specs=VMEM,
        compiler_params=PARAMS,
        cost_estimate=pl.CostEstimate(flops=1, bytes_accessed=1, transcendentals=0),
    )(band_mask, density, pick(row, last, cols))
    packed = move(packed, sizes, forward)
    local, back = pl.pallas_call(
        functools.partial(band_kernel, centre),
        out_shape=[jax.ShapeDtypeStruct((cols, cols), BF16), jax.ShapeDtypeStruct((wide, wide), BF16)],
        in_specs=[SMEM, VMEM],
        out_specs=[VMEM] * 2,
        compiler_params=PARAMS,
        cost_estimate=pl.CostEstimate(flops=1, bytes_accessed=1, transcendentals=0),
    )(band_mask, density)
    mine = pick(row, 0, cols)
    halos = [move(part, sizes, forward) for part in edges]
    rests = [
        move(after(pick(row ^ d, 0, last), edges[d - 1]), sizes, lambda i, j, k, d=d: (i, j ^ d, k))
        for d in range(1, n_row)
    ]

    whole = n_row * rows
    total, open_part = pl.pallas_call(
        functools.partial(inner_kernel, n_row, wide),
        out_shape=[jax.ShapeDtypeStruct((whole, whole), F32), jax.ShapeDtypeStruct((chunk, whole, wide), F32)],
        in_specs=[VMEM] * (2 * n_row),
        out_specs=[VMEM] * 2,
        compiler_params=PARAMS,
        cost_estimate=pl.CostEstimate(flops=1, bytes_accessed=1, transcendentals=0),
    )(mine, *rests, *edges, local)

    half = n_row * n_col // 2
    out_rows = whole // n_col
    keep, give = pl.pallas_call(
        functools.partial(outer_kernel, n_row, centre, plan, sizes),
        out_shape=[jax.ShapeDtypeStruct((half, out_rows, rows), F32)] * 2,
        in_specs=[VMEM] * (2 * n_row + 3),
        out_specs=[VMEM] * 2,
        scratch_shapes=[pltpu.VMEM((wide, wide), BF16), pltpu.VMEM((n_row, whole, rows), F32)],
        compiler_params=PARAMS,
        cost_estimate=pl.CostEstimate(flops=1, bytes_accessed=1, transcendentals=0),
    )(mine, *rests, packed, *halos, back, total, open_part)

    got = move(give, sizes, lambda i, j, k: (i ^ 1, j, k))
    pieces = keep + got
    total = jnp.where(core == 0, pieces[half - 1], 0.0)
    for n, (zero, one) in enumerate(zip(*plan)):
        def target(i, j, k):
            dr, dc = one if i % 2 else zero
            return None if (dr, dc) == (0, 0) else (i, j ^ dr, k ^ dc)

        total = total + move(pieces[n], sizes, target)
    result = total
    for d in range(2, n_ri, 2):
        result = result + move(total, sizes, lambda i, j, k, d=d: (i ^ d, j, k))
    return result + move(result, sizes, lambda i, j, k: (i ^ 1, j, k))


def solution(mesh):
    sizes = tuple(mesh.shape[axis] for axis in AXES)
    placed = (P("ri", "row", "col"), P("col", None, None), P("col", None))
    return jax.shard_map(
        functools.partial(per_device, sizes), mesh=mesh, in_specs=placed, out_specs=P("col", "row"), check_vma=False
    )
```

```python
import functools

import jax
import jax.numpy as jnp
from jax import lax
from jax.experimental import pallas as pl
from jax.experimental.pallas import tpu as pltpu
from jax.sharding import PartitionSpec as P

AXES = ("ri", "row", "col")
F32 = jnp.float32
BF16 = jnp.bfloat16
VMEM = pl.BlockSpec(memory_space=pltpu.VMEM)
HBM = pl.BlockSpec(memory_space=pltpu.HBM)
SMEM = pl.BlockSpec(memory_space=pltpu.SMEM)
PARAMS = pltpu.CompilerParams(vmem_limit_bytes=32 * 1024 * 1024)


def move(value, sizes, target):
    pairs = []
    for i in range(sizes[0]):
        for j in range(sizes[1]):
            for k in range(sizes[2]):
                to = target(i, j, k)
                if to is not None:
                    pairs.append(((i * sizes[1] + j) * sizes[2] + k, (to[0] * sizes[1] + to[1]) * sizes[2] + to[2]))
    return lax.ppermute(value, AXES, pairs)


def owned(rows, cols):
    offsets = [(a, b) for a in range(rows) for b in range(cols)]
    half = len(offsets) // 2
    first = offsets[1:half] + offsets[:1]
    return first, offsets[half:]


def times(a, b):
    return jnp.dot(a, b, preferred_element_type=F32)


def times_turned(a, b):
    return lax.dot_general(a, b, (((1,), (1,)), ((), ())), preferred_element_type=F32)


def masked(mask_ref, dens_ref, l, c):
    orb = dens_ref.shape[2]
    block = dens_ref[c, l * orb : (l + 1) * orb, :]
    return jnp.where(mask_ref[l, c] != 0, block, jnp.zeros_like(block))


def beyond(centre):
    return [(l, s) for l in range(centre) for s in range(l + 1)]


def side_by_side(parts):
    return jnp.concatenate([parts[p] for p in range(parts.shape[0])], axis=1)


def cut(tensor_ref, chunk, index, lo, size, out_ref, sem):
    return pltpu.make_async_copy(tensor_ref.at[pl.ds(index * chunk, chunk), :, pl.ds(lo, size)], out_ref, sem)


def edge_kernel(tensor_ref, *refs):
    outs, sems = refs[:-1], refs[-1]
    chunk, rows, wide = outs[0].shape
    row = lax.axis_index("row")
    copies = [
        cut(tensor_ref, chunk, row ^ (d + 1), tensor_ref.shape[2] - wide, wide, out, sems.at[d])
        for d, out in enumerate(outs)
    ]
    for copy in copies:
        copy.start()
    for copy in copies:
        copy.wait()


def pack_kernel(centre, chunk, mask_ref, dens_ref, tensor_ref, out_ref, blocks_ref, sems):
    band_count, cols, orb = dens_ref.shape
    blocks = cols // orb
    rows = tensor_ref.shape[1]
    row = lax.axis_index("row")
    core = lax.rem(lax.axis_index("ri"), 2)
    copies = []
    for p in range(chunk):
        for j in range(centre):
            n = p * centre + j
            copies.append(
                pltpu.make_async_copy(
                    tensor_ref.at[row * chunk + p, :, pl.ds(cols - (centre - j) * orb, orb)],
                    out_ref.at[pl.ds(n * rows, rows), :],
                    sems.at[n],
                )
            )
    for copy in copies:
        copy.start()
    for n, (l, s) in enumerate(beyond(centre)):
        blocks_ref[n * orb : (n + 1) * orb, :] = masked(mask_ref, dens_ref, blocks - centre + l, s - l + 2 * centre)
    half = blocks_ref.shape[0] // 2
    out_ref[chunk * centre * rows :, :] = blocks_ref[pl.ds(pl.multiple_of(core * half, half), half), :]
    for copy in copies:
        copy.wait()


def band_kernel(centre, count, mask_ref, dens_ref, tensor_ref, *refs):
    mine_ref = refs[0]
    rests = refs[1:count]
    local_ref, back_ref, sems = refs[count:]
    band_count, cols, orb = dens_ref.shape
    chunk = mine_ref.shape[0]
    blocks = cols // orb
    row = lax.axis_index("row")
    copies = [cut(tensor_ref, chunk, row, 0, cols, mine_ref, sems.at[0])]
    for d, rest_ref in enumerate(rests):
        copies.append(cut(tensor_ref, chunk, row ^ (d + 1), 0, rest_ref.shape[2], rest_ref, sems.at[d + 1]))
    for copy in copies:
        copy.start()
    local_ref[...] = jnp.zeros_like(local_ref)
    back_ref[...] = jnp.zeros_like(back_ref)
    for l in range(blocks):
        for c in range(band_count):
            s = l + c - centre
            if s < 0:
                back_ref[l * orb : (l + 1) * orb, (s + centre) * orb : (s + centre + 1) * orb] = masked(
                    mask_ref, dens_ref, l, c
                )
            elif s < blocks:
                local_ref[l * orb : (l + 1) * orb, s * orb : (s + 1) * orb] = masked(mask_ref, dens_ref, l, c)
    for copy in copies:
        copy.wait()


def inner_kernel(count, centre, *refs):
    own_ref = refs[0]
    rests = refs[1:count]
    edges = refs[count : 2 * count - 1]
    packed_ref, partner_ref, local_ref, back_ref = refs[2 * count - 1 : 2 * count + 3]
    total_ref, near_ref, behind_ref, open_ref, cross_ref, blocks_ref = refs[2 * count + 3 :]
    chunk, rows, cols = own_ref.shape
    orb = packed_ref.shape[1]
    wide = centre * orb
    core = lax.rem(lax.axis_index("ri"), 2)

    half = partner_ref.shape[0]
    blocks_ref[pl.ds(pl.multiple_of(core * half, half), half), :] = packed_ref[chunk * centre * rows :, :]
    blocks_ref[pl.ds(pl.multiple_of((1 - core) * half, half), half), :] = partner_ref[...]
    cross_ref[...] = jnp.zeros_like(cross_ref)
    for n, (l, s) in enumerate(beyond(centre)):
        cross_ref[l * orb : (l + 1) * orb, s * orb : (s + 1) * orb] = blocks_ref[n * orb : (n + 1) * orb, :]

    def turned(columns):
        return side_by_side(columns.reshape(chunk, rows, columns.shape[1]))

    halo = jnp.concatenate(
        [
            jnp.concatenate([packed_ref[(p * centre + j) * rows :][:rows] for j in range(centre)], axis=1)
            for p in range(chunk)
        ],
        axis=0,
    )
    held = [own_ref[...].reshape(chunk * rows, cols)] + [
        jnp.concatenate([rest[...], edge[...]], axis=2).reshape(chunk * rows, cols) for rest, edge in zip(rests, edges)
    ]
    near, behind, later, later_mixed = [], [], [], []
    first = None
    for d, columns in enumerate(held):
        near.append(turned(columns[:, :wide]))
        behind.append(turned(times(columns[:, :wide], back_ref[...]).astype(BF16)))
        mixed = times(columns[:, : min(cols, 2 * wide)], local_ref[: min(cols, 2 * wide), :wide])
        if d == 0:
            first = turned((mixed + times(halo, cross_ref[...])).astype(BF16))
        else:
            open_ref[d - 1] = mixed
        part, part_mixed = [], []
        for lo in range(wide, cols, wide):
            l_lo, l_hi = lo - wide, min(cols, lo + 2 * wide)
            part.append(turned(columns[:, lo : lo + wide]))
            part_mixed.append(
                turned(times(columns[:, l_lo:l_hi], local_ref[l_lo:l_hi, lo : lo + wide]).astype(BF16))
            )
        later.append(jnp.concatenate(part, axis=1))
        later_mixed.append(jnp.concatenate(part_mixed, axis=1))
    near = jnp.concatenate(near, axis=0)
    behind = jnp.concatenate(behind, axis=0)
    near_ref[...] = near
    behind_ref[...] = behind
    total_ref[...] = times_turned(jnp.concatenate(later, axis=0), jnp.concatenate(later_mixed, axis=0))
    total_ref[:, :rows] += times_turned(near, first)
    total_ref[:rows, :] += times_turned(turned(halo), behind)


def outer_kernel(count, plan, sizes, *refs):
    halos = refs[: count - 1]
    inner_ref, near_ref, behind_ref, open_ref, cross_ref, keep_ref, give_ref, kx_ref = refs[count - 1 :]
    chunk, rows, wide = halos[0].shape
    core = lax.rem(lax.axis_index("ri"), 2)
    row = lax.axis_index("row")
    col = lax.axis_index("col")
    mixed = []
    for d, halo in enumerate(halos):
        part = open_ref[d] + times(halo[...].reshape(chunk * rows, wide), cross_ref[...])
        mixed.append(side_by_side(part.astype(BF16).reshape(chunk, rows, wide)))
    columns = times_turned(near_ref[...], jnp.concatenate(mixed, axis=0))
    lines = times_turned(jnp.concatenate([side_by_side(halo[...]) for halo in halos], axis=0), behind_ref[...])
    for d in range(count):
        at = slice(d * rows, (d + 1) * rows)
        kx_ref[d, :rows] = inner_ref[:rows, at]
        kx_ref[d, rows:] = inner_ref[rows:, at] + lines[:, at]
        if d > 0:
            kx_ref[d] += columns[:, (d - 1) * rows : d * rows]
    out_rows = count * rows // sizes[2]
    per_group = rows // out_rows
    for ref, side in ((give_ref, 1 - core), (keep_ref, core)):
        for k, (zero, one) in enumerate(zip(*plan)):
            dr = jnp.where(side == 0, zero[0], one[0])
            to_col = col ^ jnp.where(side == 0, zero[1], one[1])
            start = ((to_col // per_group) ^ row) * rows + (to_col % per_group) * out_rows
            ref[k] = kx_ref[dr, pl.ds(pl.multiple_of(start, out_rows), out_rows), :]


def kernel(body, outs, in_specs, scratch=()):
    return pl.pallas_call(
        body,
        out_shape=outs,
        in_specs=in_specs,
        out_specs=[VMEM] * len(outs),
        scratch_shapes=scratch,
        compiler_params=PARAMS,
        cost_estimate=pl.CostEstimate(flops=1, bytes_accessed=1, transcendentals=0),
    )


def per_device(sizes, three_centre, density_band, band_mask):
    n_ri, n_row, n_col = sizes
    funcs, rows, cols = three_centre.shape
    band_count, orb = density_band.shape[1:]
    centre = band_count // 2
    wide = centre * orb
    chunk = funcs // n_row
    core = lax.rem(lax.axis_index("ri"), 2)
    plan = owned(n_row, n_col)
    array = jax.ShapeDtypeStruct
    sems = pltpu.SemaphoreType.DMA

    def forward(i, j, k):
        return i, j, (k + 1) % n_col

    density = jnp.transpose(density_band, (1, 0, 2))
    edges = kernel(
        edge_kernel, [array((chunk, rows, wide), BF16)] * (n_row - 1), [HBM], [sems((n_row - 1,))]
    )(three_centre)
    edges = [move(edges[d - 1], sizes, lambda i, j, k, d=d: (i, j ^ d, k)) for d in range(1, n_row)]
    half = len(beyond(centre)) * orb // 2
    own_halo = chunk * centre * rows
    (packed,) = kernel(
        functools.partial(pack_kernel, centre, chunk),
        [array((own_halo + half, orb), BF16)],
        [SMEM, VMEM, HBM],
        [pltpu.VMEM((2 * half, orb), BF16), sems((chunk * centre,))],
    )(band_mask, density, three_centre)
    packed = move(packed, sizes, forward)
    partner = move(packed[own_halo:], sizes, lambda i, j, k: (i ^ 1, j, k))
    mine, *rests, local, back = kernel(
        functools.partial(band_kernel, centre, n_row),
        [array((chunk, rows, cols), BF16)]
        + [array((chunk, rows, cols - wide), BF16)] * (n_row - 1)
        + [array((cols, cols), BF16), array((wide, wide), BF16)],
        [SMEM, VMEM, HBM],
        [sems((n_row,))],
    )(band_mask, density, three_centre)
    halos = [move(part, sizes, forward) for part in edges]
    rests = [
        move(rests[d - 1], sizes, lambda i, j, k, d=d: (i, j ^ d, k)) for d in range(1, n_row)
    ]

    whole = n_row * rows
    handed = kernel(
        functools.partial(inner_kernel, n_row, centre),
        [
            array((whole, whole), F32),
            array((whole, chunk * wide), BF16),
            array((whole, chunk * wide), BF16),
            array((n_row - 1, chunk * rows, wide), F32),
            array((wide, wide), BF16),
        ],
        [VMEM] * (2 * n_row + 3),
        [pltpu.VMEM((2 * half, orb), BF16)],
    )(mine, *rests, *edges, packed, partner, local, back)

    half = n_row * n_col // 2
    keep, give = kernel(
        functools.partial(outer_kernel, n_row, plan, sizes),
        [array((half, whole // n_col, rows), F32)] * 2,
        [VMEM] * (n_row - 1 + 5),
        [pltpu.VMEM((n_row, whole, rows), F32)],
    )(*halos, *handed)

    got = move(give, sizes, lambda i, j, k: (i ^ 1, j, k))
    pieces = keep + got
    total = jnp.where(core == 0, pieces[half - 1], 0.0)
    for n, (zero, one) in enumerate(zip(*plan)):
        def target(i, j, k):
            dr, dc = one if i % 2 else zero
            return None if (dr, dc) == (0, 0) else (i, j ^ dr, k ^ dc)

        total = total + move(pieces[n], sizes, target)
    result = total
    for d in range(2, n_ri, 2):
        result = result + move(total, sizes, lambda i, j, k, d=d: (i ^ d, j, k))
    return result + move(result, sizes, lambda i, j, k: (i ^ 1, j, k))


def solution(mesh):
    sizes = tuple(mesh.shape[axis] for axis in AXES)
    placed = (P("ri", "row", "col"), P("col", None, None), P("col", None))
    return jax.shard_map(
        functools.partial(per_device, sizes), mesh=mesh, in_specs=placed, out_specs=P("col", "row"), check_vma=False
    )
```

```python
import functools

import jax
import jax.numpy as jnp
from jax import lax
from jax.experimental import pallas as pl
from jax.experimental.pallas import tpu as pltpu
from jax.sharding import PartitionSpec as P

AXES = ("ri", "row", "col")
F32 = jnp.float32
BF16 = jnp.bfloat16
VMEM = pl.BlockSpec(memory_space=pltpu.VMEM)
HBM = pl.BlockSpec(memory_space=pltpu.HBM)
SMEM = pl.BlockSpec(memory_space=pltpu.SMEM)
PARAMS = pltpu.CompilerParams(vmem_limit_bytes=32 * 1024 * 1024)


def move(value, sizes, target):
    pairs = []
    for i in range(sizes[0]):
        for j in range(sizes[1]):
            for k in range(sizes[2]):
                to = target(i, j, k)
                if to is not None:
                    pairs.append(((i * sizes[1] + j) * sizes[2] + k, (to[0] * sizes[1] + to[1]) * sizes[2] + to[2]))
    return lax.ppermute(value, AXES, pairs)


def after(value, *earlier):
    return lax.optimization_barrier((value,) + earlier)[0]


def owned(rows, cols):
    offsets = [(a, b) for a in range(rows) for b in range(cols)]
    half = len(offsets) // 2
    first = offsets[1:half] + offsets[:1]
    return first, offsets[half:]


def times(a, b):
    return jnp.dot(a, b, preferred_element_type=F32)


def times_turned(a, b):
    return lax.dot_general(a, b, (((1,), (1,)), ((), ())), preferred_element_type=F32)


def masked(mask_ref, dens_ref, l, c):
    orb = dens_ref.shape[2]
    block = dens_ref[c, l * orb : (l + 1) * orb, :]
    return jnp.where(mask_ref[l, c] != 0, block, jnp.zeros_like(block))


def beyond(centre):
    return [(l, s) for l in range(centre) for s in range(l + 1)]


def side_by_side(parts):
    return jnp.concatenate([parts[p] for p in range(parts.shape[0])], axis=1)


def cut(tensor_ref, chunk, index, lo, size, out_ref, sem):
    return pltpu.make_async_copy(tensor_ref.at[pl.ds(index * chunk, chunk), :, pl.ds(lo, size)], out_ref, sem)


def cut_kernel(count, tensor_ref, *refs):
    lasts, mine_ref, rests, sems = refs[:count], refs[count], refs[count + 1 : -1], refs[-1]
    chunk, rows, wide = lasts[0].shape
    cols = tensor_ref.shape[2]
    row = lax.axis_index("row")
    copies = [cut(tensor_ref, chunk, row, 0, cols, mine_ref, sems.at[0])]
    for d, out in enumerate(lasts):
        copies.append(cut(tensor_ref, chunk, row ^ d, cols - wide, wide, out, sems.at[1 + d]))
    for d, out in enumerate(rests):
        copies.append(cut(tensor_ref, chunk, row ^ (d + 1), 0, cols - wide, out, sems.at[1 + count + d]))
    for copy in copies:
        copy.start()
    for copy in copies:
        copy.wait()


def blocks_kernel(centre, mask_ref, dens_ref, out_ref, blocks_ref):
    band_count, cols, orb = dens_ref.shape
    core = lax.rem(lax.axis_index("ri"), 2)
    for n, (l, s) in enumerate(beyond(centre)):
        blocks_ref[n * orb : (n + 1) * orb, :] = masked(
            mask_ref, dens_ref, cols // orb - centre + l, s - l + 2 * centre
        )
    half = out_ref.shape[0]
    out_ref[...] = blocks_ref[pl.ds(pl.multiple_of(core * half, half), half), :]


def band_kernel(centre, mask_ref, dens_ref, local_ref, back_ref):
    band_count, cols, orb = dens_ref.shape
    blocks = cols // orb
    local_ref[...] = jnp.zeros_like(local_ref)
    back_ref[...] = jnp.zeros_like(back_ref)
    for l in range(blocks):
        for c in range(band_count):
            s = l + c - centre
            if s < 0:
                back_ref[l * orb : (l + 1) * orb, (s + centre) * orb : (s + centre + 1) * orb] = masked(
                    mask_ref, dens_ref, l, c
                )
            elif s < blocks:
                local_ref[l * orb : (l + 1) * orb, s * orb : (s + 1) * orb] = masked(mask_ref, dens_ref, l, c)


def turned(columns, chunk):
    return side_by_side(columns.reshape(chunk, columns.shape[0] // chunk, columns.shape[1]))


def own_kernel(count, *refs):
    own_ref = refs[0]
    edges = refs[1:count]
    local_ref, back_ref, total_ref, near_ref, behind_ref, open_ref, later_ref, part_ref = refs[count:]
    chunk, rows, cols = own_ref.shape
    wide = back_ref.shape[0]
    own = own_ref[...].reshape(chunk * rows, cols)
    near_ref[...] = turned(own[:, :wide], chunk)
    behind_ref[...] = turned(times(own[:, :wide], back_ref[...]).astype(BF16), chunk)
    open_ref[...] = times(own, local_ref[:, :wide])
    mixed = turned(times(own, local_ref[:, wide:]).astype(BF16), chunk)
    later = [turned(own[:, wide:], chunk)]
    for d, edge in enumerate(edges):
        columns = edge[...].reshape(chunk * rows, cols - wide)
        part_ref[d] = times(columns, local_ref[wide:, :])
        later.append(turned(columns, chunk))
    later = jnp.concatenate(later, axis=0)
    later_ref[...] = later
    total_ref[...] = times_turned(later, mixed)


def inner_kernel(count, centre, *refs):
    rests = refs[: count - 1]
    halo_ref, mine_ref, partner_ref, local_ref, back_ref = refs[count - 1 : count + 4]
    own_total_ref, own_near_ref, own_behind_ref, own_open_ref, later_ref, part_ref = refs[count + 4 : count + 10]
    total_ref, near_ref, behind_ref, open_ref, cross_ref, blocks_ref = refs[count + 10 :]
    chunk, rows, wide = halo_ref.shape
    orb = mine_ref.shape[1]
    core = lax.rem(lax.axis_index("ri"), 2)

    half = partner_ref.shape[0]
    blocks_ref[pl.ds(pl.multiple_of(core * half, half), half), :] = mine_ref[...]
    blocks_ref[pl.ds(pl.multiple_of((1 - core) * half, half), half), :] = partner_ref[...]
    cross_ref[...] = jnp.zeros_like(cross_ref)
    for n, (l, s) in enumerate(beyond(centre)):
        cross_ref[l * orb : (l + 1) * orb, s * orb : (s + 1) * orb] = blocks_ref[n * orb : (n + 1) * orb, :]

    halo = halo_ref[...].reshape(chunk * rows, wide)
    first = turned((own_open_ref[...] + times(halo, cross_ref[...])).astype(BF16), chunk)
    near, behind, mixed = [own_near_ref[...]], [own_behind_ref[...]], []
    for d, rest in enumerate(rests):
        columns = rest[...].reshape(chunk * rows, wide)
        near.append(turned(columns, chunk))
        behind.append(turned(times(columns, back_ref[...]).astype(BF16), chunk))
        whole = part_ref[d] + times(columns, local_ref[:wide, :])
        open_ref[d] = whole[:, :wide]
        mixed.append(turned(whole[:, wide:].astype(BF16), chunk))
    near = jnp.concatenate(near, axis=0)
    behind = jnp.concatenate(behind, axis=0)
    near_ref[...] = near
    behind_ref[...] = behind
    total_ref[:, :rows] = own_total_ref[...] + times_turned(near, first)
    total_ref[:, rows:] = times_turned(later_ref[...], jnp.concatenate(mixed, axis=0))
    total_ref[:rows, :] += times_turned(turned(halo, chunk), behind)


def outer_kernel(count, plan, sizes, *refs):
    halos = refs[: count - 1]
    inner_ref, near_ref, behind_ref, open_ref, cross_ref, keep_ref, give_ref, kx_ref = refs[count - 1 :]
    chunk, rows, wide = halos[0].shape
    core = lax.rem(lax.axis_index("ri"), 2)
    row = lax.axis_index("row")
    col = lax.axis_index("col")
    mixed = []
    for d, halo in enumerate(halos):
        part = open_ref[d] + times(halo[...].reshape(chunk * rows, wide), cross_ref[...])
        mixed.append(side_by_side(part.astype(BF16).reshape(chunk, rows, wide)))
    columns = times_turned(near_ref[...], jnp.concatenate(mixed, axis=0))
    lines = times_turned(jnp.concatenate([side_by_side(halo[...]) for halo in halos], axis=0), behind_ref[...])
    for d in range(count):
        at = slice(d * rows, (d + 1) * rows)
        kx_ref[d, :rows] = inner_ref[:rows, at]
        kx_ref[d, rows:] = inner_ref[rows:, at] + lines[:, at]
        if d > 0:
            kx_ref[d] += columns[:, (d - 1) * rows : d * rows]
    out_rows = count * rows // sizes[2]
    per_group = rows // out_rows
    for ref, side in ((give_ref, 1 - core), (keep_ref, core)):
        for k, (zero, one) in enumerate(zip(*plan)):
            dr = jnp.where(side == 0, zero[0], one[0])
            to_col = col ^ jnp.where(side == 0, zero[1], one[1])
            start = ((to_col // per_group) ^ row) * rows + (to_col % per_group) * out_rows
            ref[k] = kx_ref[dr, pl.ds(pl.multiple_of(start, out_rows), out_rows), :]


def kernel(body, outs, in_specs, scratch=()):
    return pl.pallas_call(
        body,
        out_shape=outs,
        in_specs=in_specs,
        out_specs=[VMEM] * len(outs),
        scratch_shapes=scratch,
        compiler_params=PARAMS,
        cost_estimate=pl.CostEstimate(flops=1, bytes_accessed=1, transcendentals=0),
    )


def per_device(sizes, three_centre, density_band, band_mask):
    n_ri, n_row, n_col = sizes
    funcs, rows, cols = three_centre.shape
    band_count, orb = density_band.shape[1:]
    centre = band_count // 2
    wide = centre * orb
    chunk = funcs // n_row
    core = lax.rem(lax.axis_index("ri"), 2)
    plan = owned(n_row, n_col)
    array = jax.ShapeDtypeStruct
    sems = pltpu.SemaphoreType.DMA

    def forward(i, j, k):
        return i, j, (k + 1) % n_col

    density = jnp.transpose(density_band, (1, 0, 2))
    cuts = kernel(
        functools.partial(cut_kernel, n_row),
        [array((chunk, rows, wide), BF16)] * n_row
        + [array((chunk, rows, cols), BF16)]
        + [array((chunk, rows, cols - wide), BF16)] * (n_row - 1),
        [HBM],
        [sems((2 * n_row,))],
    )(three_centre)
    halo, edges, mine, rests = cuts[0], cuts[1:n_row], cuts[n_row], cuts[n_row + 1 :]
    halo = move(halo, sizes, forward)
    edges = [move(edges[d - 1], sizes, lambda i, j, k, d=d: (i, j ^ d, k)) for d in range(1, n_row)]
    half = len(beyond(centre)) * orb // 2
    (blocks,) = kernel(
        functools.partial(blocks_kernel, centre),
        [array((half, orb), BF16)],
        [SMEM, VMEM],
        [pltpu.VMEM((2 * half, orb), BF16)],
    )(band_mask, density)
    blocks = move(blocks, sizes, forward)
    partner = move(blocks, sizes, lambda i, j, k: (i ^ 1, j, k))
    local, back = kernel(
        functools.partial(band_kernel, centre),
        [array((cols, cols), BF16), array((wide, wide), BF16)],
        [SMEM, VMEM],
    )(band_mask, density)
    halos = [move(after(part, blocks), sizes, forward) for part in edges]
    rests = [
        move(after(rests[d - 1], edges[d - 1]), sizes, lambda i, j, k, d=d: (i, j ^ d, k))
        for d in range(1, n_row)
    ]

    whole = n_row * rows
    side = chunk * wide
    first_terms = kernel(
        functools.partial(own_kernel, n_row),
        [
            array((whole, rows), F32),
            array((rows, side), BF16),
            array((rows, side), BF16),
            array((chunk * rows, wide), F32),
            array((whole, chunk * (cols - wide)), BF16),
            array((n_row - 1, chunk * rows, cols), F32),
        ],
        [VMEM] * (n_row + 2),
    )(mine, *edges, local, back)
    handed = kernel(
        functools.partial(inner_kernel, n_row, centre),
        [
            array((whole, whole), F32),
            array((whole, side), BF16),
            array((whole, side), BF16),
            array((n_row - 1, chunk * rows, wide), F32),
            array((wide, wide), BF16),
        ],
        [VMEM] * (n_row + 10),
        [pltpu.VMEM((2 * half, orb), BF16)],
    )(*rests, halo, blocks, partner, local, back, *first_terms)

    half = n_row * n_col // 2
    keep, give = kernel(
        functools.partial(outer_kernel, n_row, plan, sizes),
        [array((half, whole // n_col, rows), F32)] * 2,
        [VMEM] * (n_row - 1 + 5),
        [pltpu.VMEM((n_row, whole, rows), F32)],
    )(*halos, *handed)

    got = move(give, sizes, lambda i, j, k: (i ^ 1, j, k))
    pieces = keep + got
    total = jnp.where(core == 0, pieces[half - 1], 0.0)
    for n, (zero, one) in enumerate(zip(*plan)):
        def target(i, j, k):
            dr, dc = one if i % 2 else zero
            return None if (dr, dc) == (0, 0) else (i, j ^ dr, k ^ dc)

        total = total + move(pieces[n], sizes, target)
    result = total
    for d in range(2, n_ri, 2):
        result = result + move(total, sizes, lambda i, j, k, d=d: (i ^ d, j, k))
    return result + move(result, sizes, lambda i, j, k: (i ^ 1, j, k))


def solution(mesh):
    sizes = tuple(mesh.shape[axis] for axis in AXES)
    placed = (P("ri", "row", "col"), P("col", None, None), P("col", None))
    return jax.shard_map(
        functools.partial(per_device, sizes), mesh=mesh, in_specs=placed, out_specs=P("col", "row"), check_vma=False
    )
```

```python
import functools

import jax
import jax.numpy as jnp
from jax import lax
from jax.experimental import pallas as pl
from jax.experimental.pallas import tpu as pltpu
from jax.sharding import PartitionSpec as P

AXES = ("ri", "row", "col")
F32 = jnp.float32
BF16 = jnp.bfloat16
VMEM = pl.BlockSpec(memory_space=pltpu.VMEM)
HBM = pl.BlockSpec(memory_space=pltpu.HBM)
SMEM = pl.BlockSpec(memory_space=pltpu.SMEM)
PARAMS = pltpu.CompilerParams(vmem_limit_bytes=32 * 1024 * 1024)


def move(value, sizes, target):
    pairs = []
    for i in range(sizes[0]):
        for j in range(sizes[1]):
            for k in range(sizes[2]):
                to = target(i, j, k)
                if to is not None:
                    pairs.append(((i * sizes[1] + j) * sizes[2] + k, (to[0] * sizes[1] + to[1]) * sizes[2] + to[2]))
    return lax.ppermute(value, AXES, pairs)


def after(value, *earlier):
    return lax.optimization_barrier((value,) + earlier)[0]


def owned(rows, cols):
    sides = ([], [])
    for a in range(rows):
        for b in range(cols):
            sides[b if b < 2 else (a + b + 1) % 2].append((a, b))
    plan = []
    for side in sides:
        side = sorted(side, key=lambda at: (at[0] + at[1], at[0]))
        far = min(side, key=lambda at: (-at[0] - at[1], at[0]))
        plan.append([far] + [at for at in side if at != far])
    return plan


def times(a, b):
    return jnp.dot(a, b, preferred_element_type=F32)


def times_turned(a, b):
    return lax.dot_general(a, b, (((1,), (1,)), ((), ())), preferred_element_type=F32)


def masked(mask_ref, dens_ref, l, c):
    orb = dens_ref.shape[2]
    block = dens_ref[c, l * orb : (l + 1) * orb, :]
    return jnp.where(mask_ref[l, c] != 0, block, jnp.zeros_like(block))


def beyond(centre):
    return [(l, s) for l in range(centre) for s in range(l + 1)]


def side_by_side(parts):
    return jnp.concatenate([parts[p] for p in range(parts.shape[0])], axis=1)


def cut(tensor_ref, chunk, index, lo, size, out_ref, sem):
    return pltpu.make_async_copy(tensor_ref.at[pl.ds(index * chunk, chunk), :, pl.ds(lo, size)], out_ref, sem)


def cut_kernel(count, tensor_ref, *refs):
    lasts, mine_ref, rests, sems = refs[:count], refs[count], refs[count + 1 : -1], refs[-1]
    chunk, rows, wide = lasts[0].shape
    cols = tensor_ref.shape[2]
    row = lax.axis_index("row")
    copies = [cut(tensor_ref, chunk, row, 0, cols, mine_ref, sems.at[0])]
    for d, out in enumerate(lasts):
        copies.append(cut(tensor_ref, chunk, row ^ d, cols - wide, wide, out, sems.at[1 + d]))
    for d, out in enumerate(rests):
        copies.append(cut(tensor_ref, chunk, row ^ (d + 1), 0, cols - wide, out, sems.at[1 + count + d]))
    for copy in copies:
        copy.start()
    for copy in copies:
        copy.wait()


def blocks_kernel(centre, mask_ref, dens_ref, out_ref, blocks_ref):
    band_count, cols, orb = dens_ref.shape
    core = lax.rem(lax.axis_index("ri"), 2)
    for n, (l, s) in enumerate(beyond(centre)):
        blocks_ref[n * orb : (n + 1) * orb, :] = masked(
            mask_ref, dens_ref, cols // orb - centre + l, s - l + 2 * centre
        )
    half = out_ref.shape[0]
    out_ref[...] = blocks_ref[pl.ds(pl.multiple_of(core * half, half), half), :]


def band_kernel(centre, mask_ref, dens_ref, local_ref, back_ref):
    band_count, cols, orb = dens_ref.shape
    blocks = cols // orb
    local_ref[...] = jnp.zeros_like(local_ref)
    back_ref[...] = jnp.zeros_like(back_ref)
    for l in range(blocks):
        for c in range(band_count):
            s = l + c - centre
            if s < 0:
                back_ref[l * orb : (l + 1) * orb, (s + centre) * orb : (s + centre + 1) * orb] = masked(
                    mask_ref, dens_ref, l, c
                )
            elif s < blocks:
                local_ref[l * orb : (l + 1) * orb, s * orb : (s + 1) * orb] = masked(mask_ref, dens_ref, l, c)


def turned(columns, chunk):
    return side_by_side(columns.reshape(chunk, columns.shape[0] // chunk, columns.shape[1]))


def own_kernel(count, *refs):
    own_ref = refs[0]
    edges = refs[1:count]
    local_ref, back_ref, total_ref, near_ref, behind_ref, open_ref, later_ref, part_ref = refs[count:]
    chunk, rows, cols = own_ref.shape
    wide = back_ref.shape[0]
    own = own_ref[...].reshape(chunk * rows, cols)
    near_ref[...] = turned(own[:, :wide], chunk)
    behind_ref[...] = turned(times(own[:, :wide], back_ref[...]).astype(BF16), chunk)
    open_ref[...] = times(own, local_ref[:, :wide])
    mixed = turned(times(own, local_ref[:, wide:]).astype(BF16), chunk)
    later = [turned(own[:, wide:], chunk)]
    for d, edge in enumerate(edges):
        columns = edge[...].reshape(chunk * rows, cols - wide)
        part_ref[d] = times(columns, local_ref[wide:, :])
        later.append(turned(columns, chunk))
    later = jnp.concatenate(later, axis=0)
    later_ref[...] = later
    total_ref[...] = times_turned(later, mixed)


def inner_kernel(count, centre, *refs):
    rests = refs[: count - 1]
    halo_ref, mine_ref, partner_ref, local_ref, back_ref = refs[count - 1 : count + 4]
    own_total_ref, own_near_ref, own_behind_ref, own_open_ref, later_ref, part_ref = refs[count + 4 : count + 10]
    total_ref, near_ref, behind_ref, open_ref, cross_ref, blocks_ref = refs[count + 10 :]
    chunk, rows, wide = halo_ref.shape
    orb = mine_ref.shape[1]
    core = lax.rem(lax.axis_index("ri"), 2)

    half = partner_ref.shape[0]
    blocks_ref[pl.ds(pl.multiple_of(core * half, half), half), :] = mine_ref[...]
    blocks_ref[pl.ds(pl.multiple_of((1 - core) * half, half), half), :] = partner_ref[...]
    cross_ref[...] = jnp.zeros_like(cross_ref)
    for n, (l, s) in enumerate(beyond(centre)):
        cross_ref[l * orb : (l + 1) * orb, s * orb : (s + 1) * orb] = blocks_ref[n * orb : (n + 1) * orb, :]

    halo = halo_ref[...].reshape(chunk * rows, wide)
    first = turned((own_open_ref[...] + times(halo, cross_ref[...])).astype(BF16), chunk)
    near, behind, mixed = [own_near_ref[...]], [own_behind_ref[...]], []
    for d, rest in enumerate(rests):
        columns = rest[...].reshape(chunk * rows, wide)
        near.append(turned(columns, chunk))
        behind.append(turned(times(columns, back_ref[...]).astype(BF16), chunk))
        whole = part_ref[d] + times(columns, local_ref[:wide, :])
        open_ref[d] = whole[:, :wide]
        mixed.append(turned(whole[:, wide:].astype(BF16), chunk))
    near = jnp.concatenate(near, axis=0)
    behind = jnp.concatenate(behind, axis=0)
    near_ref[...] = near
    behind_ref[...] = behind
    total_ref[:, :rows] = own_total_ref[...] + times_turned(near, first)
    total_ref[:, rows:] = times_turned(later_ref[...], jnp.concatenate(mixed, axis=0))
    total_ref[:rows, :] += times_turned(turned(halo, chunk), behind)


def outer_kernel(count, plan, sizes, *refs):
    halos = refs[: count - 1]
    inner_ref, near_ref, behind_ref, open_ref, cross_ref, keep_ref, give_ref, kx_ref = refs[count - 1 :]
    chunk, rows, wide = halos[0].shape
    core = lax.rem(lax.axis_index("ri"), 2)
    row = lax.axis_index("row")
    col = lax.axis_index("col")
    mixed = []
    for d, halo in enumerate(halos):
        part = open_ref[d] + times(halo[...].reshape(chunk * rows, wide), cross_ref[...])
        mixed.append(side_by_side(part.astype(BF16).reshape(chunk, rows, wide)))
    columns = times_turned(near_ref[...], jnp.concatenate(mixed, axis=0))
    lines = times_turned(jnp.concatenate([side_by_side(halo[...]) for halo in halos], axis=0), behind_ref[...])
    for d in range(count):
        at = slice(d * rows, (d + 1) * rows)
        kx_ref[d, :rows] = inner_ref[:rows, at]
        kx_ref[d, rows:] = inner_ref[rows:, at] + lines[:, at]
        if d > 0:
            kx_ref[d] += columns[:, (d - 1) * rows : d * rows]
    out_rows = count * rows // sizes[2]
    per_group = rows // out_rows
    for ref, side in ((give_ref, 1 - core), (keep_ref, core)):
        for k, (zero, one) in enumerate(zip(*plan)):
            dr = jnp.where(side == 0, zero[0], one[0])
            to_col = col ^ jnp.where(side == 0, zero[1], one[1])
            start = ((to_col // per_group) ^ row) * rows + (to_col % per_group) * out_rows
            ref[k] = kx_ref[dr, pl.ds(pl.multiple_of(start, out_rows), out_rows), :]


def kernel(body, outs, in_specs, scratch=()):
    return pl.pallas_call(
        body,
        out_shape=outs,
        in_specs=in_specs,
        out_specs=[VMEM] * len(outs),
        scratch_shapes=scratch,
        compiler_params=PARAMS,
        cost_estimate=pl.CostEstimate(flops=1, bytes_accessed=1, transcendentals=0),
    )


def per_device(sizes, three_centre, density_band, band_mask):
    n_ri, n_row, n_col = sizes
    funcs, rows, cols = three_centre.shape
    band_count, orb = density_band.shape[1:]
    centre = band_count // 2
    wide = centre * orb
    chunk = funcs // n_row
    core = lax.rem(lax.axis_index("ri"), 2)
    plan = owned(n_row, n_col)
    array = jax.ShapeDtypeStruct
    sems = pltpu.SemaphoreType.DMA

    def forward(i, j, k):
        return i, j, (k + 1) % n_col

    density = jnp.transpose(density_band, (1, 0, 2))
    cuts = kernel(
        functools.partial(cut_kernel, n_row),
        [array((chunk, rows, wide), BF16)] * n_row
        + [array((chunk, rows, cols), BF16)]
        + [array((chunk, rows, cols - wide), BF16)] * (n_row - 1),
        [HBM],
        [sems((2 * n_row,))],
    )(three_centre)
    halo, edges, mine, rests = cuts[0], cuts[1:n_row], cuts[n_row], cuts[n_row + 1 :]
    halo = move(halo, sizes, forward)
    edges = [move(edges[d - 1], sizes, lambda i, j, k, d=d: (i, j ^ d, k)) for d in range(1, n_row)]
    half = len(beyond(centre)) * orb // 2
    (blocks,) = kernel(
        functools.partial(blocks_kernel, centre),
        [array((half, orb), BF16)],
        [SMEM, VMEM],
        [pltpu.VMEM((2 * half, orb), BF16)],
    )(band_mask, density)
    blocks = move(blocks, sizes, forward)
    partner = move(blocks, sizes, lambda i, j, k: (i ^ 1, j, k))
    local, back = kernel(
        functools.partial(band_kernel, centre),
        [array((cols, cols), BF16), array((wide, wide), BF16)],
        [SMEM, VMEM],
    )(band_mask, density)
    halos = [move(after(part, blocks), sizes, forward) for part in edges]
    rests = [
        move(after(rests[d - 1], edges[d - 1]), sizes, lambda i, j, k, d=d: (i, j ^ d, k))
        for d in range(1, n_row)
    ]

    whole = n_row * rows
    side = chunk * wide
    first_terms = kernel(
        functools.partial(own_kernel, n_row),
        [
            array((whole, rows), F32),
            array((rows, side), BF16),
            array((rows, side), BF16),
            array((chunk * rows, wide), F32),
            array((whole, chunk * (cols - wide)), BF16),
            array((n_row - 1, chunk * rows, cols), F32),
        ],
        [VMEM] * (n_row + 2),
    )(mine, *edges, local, back)
    handed = kernel(
        functools.partial(inner_kernel, n_row, centre),
        [
            array((whole, whole), F32),
            array((whole, side), BF16),
            array((whole, side), BF16),
            array((n_row - 1, chunk * rows, wide), F32),
            array((wide, wide), BF16),
        ],
        [VMEM] * (n_row + 10),
        [pltpu.VMEM((2 * half, orb), BF16)],
    )(*rests, halo, blocks, partner, local, back, *first_terms)

    half = n_row * n_col // 2
    keep, give = kernel(
        functools.partial(outer_kernel, n_row, plan, sizes),
        [array((half, whole // n_col, rows), F32)] * 2,
        [VMEM] * (n_row - 1 + 5),
        [pltpu.VMEM((n_row, whole, rows), F32)],
    )(*halos, *handed)

    got = move(give, sizes, lambda i, j, k: (i ^ 1, j, k))
    pieces = keep + got
    total = jnp.where(core == 0, pieces[plan[0].index((0, 0))], 0.0)
    for n, (zero, one) in enumerate(zip(*plan)):
        def target(i, j, k):
            dr, dc = one if i % 2 else zero
            return None if (dr, dc) == (0, 0) else (i, j ^ dr, k ^ dc)

        total = total + move(pieces[n], sizes, target)
    result = total
    for d in range(2, n_ri, 2):
        result = result + move(total, sizes, lambda i, j, k, d=d: (i ^ d, j, k))
    return result + move(result, sizes, lambda i, j, k: (i ^ 1, j, k))


def solution(mesh):
    sizes = tuple(mesh.shape[axis] for axis in AXES)
    placed = (P("ri", "row", "col"), P("col", None, None), P("col", None))
    return jax.shard_map(
        functools.partial(per_device, sizes), mesh=mesh, in_specs=placed, out_specs=P("col", "row"), check_vma=False
    )
```

```python
import functools

import jax
import jax.numpy as jnp
from jax import lax
from jax.experimental import pallas as pl
from jax.experimental.pallas import tpu as pltpu
from jax.sharding import PartitionSpec as P

AXES = ("ri", "row", "col")
F32 = jnp.float32
BF16 = jnp.bfloat16
VMEM = pl.BlockSpec(memory_space=pltpu.VMEM)
HBM = pl.BlockSpec(memory_space=pltpu.HBM)
SMEM = pl.BlockSpec(memory_space=pltpu.SMEM)
PARAMS = pltpu.CompilerParams(vmem_limit_bytes=32 * 1024 * 1024)


def move(value, sizes, target):
    pairs = []
    for i in range(sizes[0]):
        for j in range(sizes[1]):
            for k in range(sizes[2]):
                to = target(i, j, k)
                if to is not None:
                    pairs.append(((i * sizes[1] + j) * sizes[2] + k, (to[0] * sizes[1] + to[1]) * sizes[2] + to[2]))
    return lax.ppermute(value, AXES, pairs)


def after(value, *earlier):
    return lax.optimization_barrier((value,) + earlier)[0]


def owned(rows, cols):
    sides = ([], [])
    for a in range(rows):
        for b in range(cols):
            sides[b if b < 2 else (a + b + 1) % 2].append((a, b))
    plan = []
    for side in sides:
        side = sorted(side, key=lambda at: (at[0] + at[1], at[0]))
        far = min(side, key=lambda at: (-at[0] - at[1], at[0]))
        plan.append([far] + [at for at in side if at != far])
    return plan


def times(a, b):
    return jnp.dot(a, b, preferred_element_type=F32)


def times_turned(a, b):
    return lax.dot_general(a, b, (((1,), (1,)), ((), ())), preferred_element_type=F32)


def masked(mask_ref, dens_ref, l, c):
    orb = dens_ref.shape[2]
    kept = mask_ref[l : l + 1, c : c + 1].astype(F32)
    return (dens_ref[c, l * orb : (l + 1) * orb, :].astype(F32) * kept).astype(BF16)


def beyond(centre):
    return [(l, s) for l in range(centre) for s in range(l + 1)]


def side_by_side(parts):
    return jnp.concatenate([parts[p] for p in range(parts.shape[0])], axis=1)


def cut(tensor_ref, chunk, index, lo, size, out_ref, sem):
    return pltpu.make_async_copy(tensor_ref.at[pl.ds(index * chunk, chunk), :, pl.ds(lo, size)], out_ref, sem)


def cut_kernel(count, tensor_ref, *refs):
    lasts, mine_ref, rests, sems = refs[:count], refs[count], refs[count + 1 : -1], refs[-1]
    chunk, rows, wide = lasts[0].shape
    cols = tensor_ref.shape[2]
    row = lax.axis_index("row")
    copies = [cut(tensor_ref, chunk, row, 0, cols, mine_ref, sems.at[0])]
    for d, out in enumerate(lasts):
        copies.append(cut(tensor_ref, chunk, row ^ d, cols - wide, wide, out, sems.at[1 + d]))
    for d, out in enumerate(rests):
        copies.append(cut(tensor_ref, chunk, row ^ (d + 1), 0, cols - wide, out, sems.at[1 + count + d]))
    for copy in copies:
        copy.start()
    for copy in copies:
        copy.wait()


def blocks_kernel(centre, mask_ref, dens_ref, out_ref, blocks_ref):
    band_count, cols, orb = dens_ref.shape
    core = lax.rem(lax.axis_index("ri"), 2)
    for n, (l, s) in enumerate(beyond(centre)):
        blocks_ref[n * orb : (n + 1) * orb, :] = masked(
            mask_ref, dens_ref, cols // orb - centre + l, s - l + 2 * centre
        )
    half = out_ref.shape[0]
    out_ref[...] = blocks_ref[pl.ds(pl.multiple_of(core * half, half), half), :]


def band_kernel(centre, mask_ref, dens_ref, local_ref, back_ref):
    band_count, cols, orb = dens_ref.shape
    blocks = cols // orb
    local_ref[...] = jnp.zeros_like(local_ref)
    back_ref[...] = jnp.zeros_like(back_ref)
    for l in range(blocks):
        for c in range(band_count):
            s = l + c - centre
            if s < 0:
                back_ref[l * orb : (l + 1) * orb, (s + centre) * orb : (s + centre + 1) * orb] = masked(
                    mask_ref, dens_ref, l, c
                )
            elif s < blocks:
                local_ref[l * orb : (l + 1) * orb, s * orb : (s + 1) * orb] = masked(mask_ref, dens_ref, l, c)


def turned(columns, chunk):
    return side_by_side(columns.reshape(chunk, columns.shape[0] // chunk, columns.shape[1]))


def own_kernel(own_ref, local_ref, back_ref, near_ref, behind_ref, open_ref, later_ref, mixed_ref):
    chunk, rows, cols = own_ref.shape
    wide = back_ref.shape[0]
    own = own_ref[...].reshape(chunk * rows, cols)
    near_ref[...] = turned(own[:, :wide], chunk)
    behind_ref[...] = turned(times(own[:, :wide], back_ref[...]).astype(BF16), chunk)
    open_ref[...] = times(own, local_ref[:, :wide])
    mixed_ref[...] = turned(times(own, local_ref[:, wide:]).astype(BF16), chunk)
    later_ref[...] = turned(own[:, wide:], chunk)


def edge_kernel(count, *refs):
    edges = refs[: count - 1]
    local_ref, own_later_ref, mixed_ref, total_ref, later_ref, part_ref = refs[count - 1 :]
    chunk, rows, wide = edges[0].shape
    later = [own_later_ref[...]]
    for d, edge in enumerate(edges):
        columns = edge[...].reshape(chunk * rows, wide)
        part_ref[d] = times(columns, local_ref[local_ref.shape[0] - wide :, :])
        later.append(turned(columns, chunk))
    later = jnp.concatenate(later, axis=0)
    later_ref[...] = later
    total_ref[...] = times_turned(later, mixed_ref[...])


def inner_kernel(count, centre, *refs):
    rests = refs[: count - 1]
    halo_ref, mine_ref, partner_ref, local_ref, back_ref = refs[count - 1 : count + 4]
    own_total_ref, own_near_ref, own_behind_ref, own_open_ref, later_ref, part_ref = refs[count + 4 : count + 10]
    total_ref, near_ref, behind_ref, open_ref, cross_ref, blocks_ref = refs[count + 10 :]
    chunk, rows, wide = halo_ref.shape
    orb = mine_ref.shape[1]
    core = lax.rem(lax.axis_index("ri"), 2)

    half = partner_ref.shape[0]
    blocks_ref[pl.ds(pl.multiple_of(core * half, half), half), :] = mine_ref[...]
    blocks_ref[pl.ds(pl.multiple_of((1 - core) * half, half), half), :] = partner_ref[...]
    cross_ref[...] = jnp.zeros_like(cross_ref)
    for n, (l, s) in enumerate(beyond(centre)):
        cross_ref[l * orb : (l + 1) * orb, s * orb : (s + 1) * orb] = blocks_ref[n * orb : (n + 1) * orb, :]

    halo = halo_ref[...].reshape(chunk * rows, wide)
    first = turned((own_open_ref[...] + times(halo, cross_ref[...])).astype(BF16), chunk)
    near, behind, mixed = [own_near_ref[...]], [own_behind_ref[...]], []
    for d, rest in enumerate(rests):
        columns = rest[...].reshape(chunk * rows, wide)
        near.append(turned(columns, chunk))
        behind.append(turned(times(columns, back_ref[...]).astype(BF16), chunk))
        whole = part_ref[d] + times(columns, local_ref[:wide, :])
        open_ref[d] = whole[:, :wide]
        mixed.append(turned(whole[:, wide:].astype(BF16), chunk))
    near = jnp.concatenate(near, axis=0)
    behind = jnp.concatenate(behind, axis=0)
    near_ref[...] = near
    behind_ref[...] = behind
    total_ref[:, :rows] = own_total_ref[...] + times_turned(near, first)
    total_ref[:, rows:] = times_turned(later_ref[...], jnp.concatenate(mixed, axis=0))
    total_ref[:rows, :] += times_turned(turned(halo, chunk), behind)


def outer_kernel(count, plan, sizes, *refs):
    halos = refs[: count - 1]
    inner_ref, near_ref, behind_ref, open_ref, cross_ref, keep_ref, give_ref, kx_ref = refs[count - 1 :]
    chunk, rows, wide = halos[0].shape
    core = lax.rem(lax.axis_index("ri"), 2)
    row = lax.axis_index("row")
    col = lax.axis_index("col")
    mixed = []
    for d, halo in enumerate(halos):
        part = open_ref[d] + times(halo[...].reshape(chunk * rows, wide), cross_ref[...])
        mixed.append(side_by_side(part.astype(BF16).reshape(chunk, rows, wide)))
    columns = times_turned(near_ref[...], jnp.concatenate(mixed, axis=0))
    lines = times_turned(jnp.concatenate([side_by_side(halo[...]) for halo in halos], axis=0), behind_ref[...])
    for d in range(count):
        at = slice(d * rows, (d + 1) * rows)
        kx_ref[d, :rows] = inner_ref[:rows, at]
        kx_ref[d, rows:] = inner_ref[rows:, at] + lines[:, at]
        if d > 0:
            kx_ref[d] += columns[:, (d - 1) * rows : d * rows]
    out_rows = count * rows // sizes[2]
    per_group = rows // out_rows
    for ref, side in ((give_ref, 1 - core), (keep_ref, core)):
        for k, (zero, one) in enumerate(zip(*plan)):
            dr = jnp.where(side == 0, zero[0], one[0])
            to_col = col ^ jnp.where(side == 0, zero[1], one[1])
            start = ((to_col // per_group) ^ row) * rows + (to_col % per_group) * out_rows
            ref[k] = kx_ref[dr, pl.ds(pl.multiple_of(start, out_rows), out_rows), :]


def kernel(body, outs, in_specs, scratch=()):
    return pl.pallas_call(
        body,
        out_shape=outs,
        in_specs=in_specs,
        out_specs=[VMEM] * len(outs),
        scratch_shapes=scratch,
        compiler_params=PARAMS,
        cost_estimate=pl.CostEstimate(flops=1, bytes_accessed=1, transcendentals=0),
    )


def per_device(sizes, three_centre, density_band, band_mask):
    n_ri, n_row, n_col = sizes
    funcs, rows, cols = three_centre.shape
    band_count, orb = density_band.shape[1:]
    centre = band_count // 2
    wide = centre * orb
    chunk = funcs // n_row
    core = lax.rem(lax.axis_index("ri"), 2)
    plan = owned(n_row, n_col)
    array = jax.ShapeDtypeStruct
    sems = pltpu.SemaphoreType.DMA

    def forward(i, j, k):
        return i, j, (k + 1) % n_col

    density = jnp.transpose(density_band, (1, 0, 2))
    cuts = kernel(
        functools.partial(cut_kernel, n_row),
        [array((chunk, rows, wide), BF16)] * n_row
        + [array((chunk, rows, cols), BF16)]
        + [array((chunk, rows, cols - wide), BF16)] * (n_row - 1),
        [HBM],
        [sems((2 * n_row,))],
    )(three_centre)
    halo, edges, mine, rests = cuts[0], cuts[1:n_row], cuts[n_row], cuts[n_row + 1 :]
    halo = move(halo, sizes, forward)
    edges = [move(edges[d - 1], sizes, lambda i, j, k, d=d: (i, j ^ d, k)) for d in range(1, n_row)]
    half = len(beyond(centre)) * orb // 2
    (blocks,) = kernel(
        functools.partial(blocks_kernel, centre),
        [array((half, orb), BF16)],
        [VMEM, VMEM],
        [pltpu.VMEM((2 * half, orb), BF16)],
    )(band_mask, density)
    blocks = move(blocks, sizes, forward)
    partner = move(blocks, sizes, lambda i, j, k: (i ^ 1, j, k))
    local, back = kernel(
        functools.partial(band_kernel, centre),
        [array((cols, cols), BF16), array((wide, wide), BF16)],
        [VMEM, VMEM],
    )(band_mask, after(density, blocks))
    whole = n_row * rows
    side = chunk * wide
    *own, own_later, mixed = kernel(
        own_kernel,
        [
            array((rows, side), BF16),
            array((rows, side), BF16),
            array((chunk * rows, wide), F32),
            array((rows, chunk * (cols - wide)), BF16),
            array((rows, chunk * (cols - wide)), BF16),
        ],
        [VMEM] * 3,
    )(mine, local, back)
    halos = [move(after(part, blocks), sizes, forward) for part in edges]
    rests = [
        move(after(rests[d - 1], mixed), sizes, lambda i, j, k, d=d: (i, j ^ d, k))
        for d in range(1, n_row)
    ]

    total, later, part = kernel(
        functools.partial(edge_kernel, n_row),
        [
            array((whole, rows), F32),
            array((whole, chunk * (cols - wide)), BF16),
            array((n_row - 1, chunk * rows, cols), F32),
        ],
        [VMEM] * (n_row + 2),
    )(*edges, local, own_later, mixed)
    first_terms = [total, *own, later, part]
    handed = kernel(
        functools.partial(inner_kernel, n_row, centre),
        [
            array((whole, whole), F32),
            array((whole, side), BF16),
            array((whole, side), BF16),
            array((n_row - 1, chunk * rows, wide), F32),
            array((wide, wide), BF16),
        ],
        [VMEM] * (n_row + 10),
        [pltpu.VMEM((2 * half, orb), BF16)],
    )(*rests, halo, blocks, partner, local, back, *first_terms)

    half = n_row * n_col // 2
    keep, give = kernel(
        functools.partial(outer_kernel, n_row, plan, sizes),
        [array((half, whole // n_col, rows), F32)] * 2,
        [VMEM] * (n_row - 1 + 5),
        [pltpu.VMEM((n_row, whole, rows), F32)],
    )(*halos, *handed)

    got = move(give, sizes, lambda i, j, k: (i ^ 1, j, k))
    pieces = keep + got
    total = jnp.where(core == 0, pieces[plan[0].index((0, 0))], 0.0)
    for n, (zero, one) in enumerate(zip(*plan)):
        def target(i, j, k):
            dr, dc = one if i % 2 else zero
            return None if (dr, dc) == (0, 0) else (i, j ^ dr, k ^ dc)

        total = total + move(pieces[n], sizes, target)
    result = total
    for d in range(2, n_ri, 2):
        result = result + move(total, sizes, lambda i, j, k, d=d: (i ^ d, j, k))
    return result + move(result, sizes, lambda i, j, k: (i ^ 1, j, k))


def solution(mesh):
    sizes = tuple(mesh.shape[axis] for axis in AXES)
    placed = (P("ri", "row", "col"), P("col", None, None), P("col", None))
    return jax.shard_map(
        functools.partial(per_device, sizes), mesh=mesh, in_specs=placed, out_specs=P("col", "row"), check_vma=False
    )
```

```python
import functools

import jax
import jax.numpy as jnp
from jax import lax
from jax.experimental import pallas as pl
from jax.experimental.pallas import tpu as pltpu
from jax.sharding import PartitionSpec as P

AXES = ("ri", "row", "col")
F32 = jnp.float32
BF16 = jnp.bfloat16
VMEM = pl.BlockSpec(memory_space=pltpu.VMEM)
HBM = pl.BlockSpec(memory_space=pltpu.HBM)
SMEM = pl.BlockSpec(memory_space=pltpu.SMEM)
PARAMS = pltpu.CompilerParams(vmem_limit_bytes=32 * 1024 * 1024)


def move(value, sizes, target):
    pairs = []
    for i in range(sizes[0]):
        for j in range(sizes[1]):
            for k in range(sizes[2]):
                to = target(i, j, k)
                if to is not None:
                    pairs.append(((i * sizes[1] + j) * sizes[2] + k, (to[0] * sizes[1] + to[1]) * sizes[2] + to[2]))
    return lax.ppermute(value, AXES, pairs)


def after(value, *earlier):
    return lax.optimization_barrier((value,) + earlier)[0]


def owned(rows, cols):
    sides = ([], [])
    for a in range(rows):
        for b in range(cols):
            sides[b if b < 2 else (a + b + 1) % 2].append((a, b))
    plan = []
    for side in sides:
        side = sorted(side, key=lambda at: (at[0] + at[1], at[0]))
        far = min(side, key=lambda at: (-at[0] - at[1], at[0]))
        plan.append([far] + [at for at in side if at != far])
    return plan


def times(a, b):
    return jnp.dot(a, b, preferred_element_type=F32)


def times_turned(a, b):
    return lax.dot_general(a, b, (((1,), (1,)), ((), ())), preferred_element_type=F32)


def masked(mask_ref, dens_ref, l, c):
    orb = dens_ref.shape[2]
    kept = mask_ref[l : l + 1, c : c + 1].astype(F32)
    return (dens_ref[c, l * orb : (l + 1) * orb, :].astype(F32) * kept).astype(BF16)


def beyond(centre):
    return [(l, s) for l in range(centre) for s in range(l + 1)]


def side_by_side(parts):
    return jnp.concatenate([parts[p] for p in range(parts.shape[0])], axis=1)


def cut(tensor_ref, chunk, index, lo, size, out_ref, sem):
    return pltpu.make_async_copy(tensor_ref.at[pl.ds(index * chunk, chunk), :, pl.ds(lo, size)], out_ref, sem)


def cut_kernel(count, tensor_ref, *refs):
    lasts, mine_ref, rests, sems = refs[:count], refs[count], refs[count + 1 : -1], refs[-1]
    chunk, rows, wide = lasts[0].shape
    cols = tensor_ref.shape[2]
    row = lax.axis_index("row")
    copies = [cut(tensor_ref, chunk, row, 0, cols, mine_ref, sems.at[0])]
    for d, out in enumerate(lasts):
        copies.append(cut(tensor_ref, chunk, row ^ d, cols - wide, wide, out, sems.at[1 + d]))
    for d, out in enumerate(rests):
        copies.append(cut(tensor_ref, chunk, row ^ (d + 1), 0, cols - wide, out, sems.at[1 + count + d]))
    for copy in copies:
        copy.start()
    for copy in copies:
        copy.wait()


def blocks_kernel(centre, mask_ref, dens_ref, out_ref, blocks_ref):
    band_count, cols, orb = dens_ref.shape
    core = lax.rem(lax.axis_index("ri"), 2)
    for n, (l, s) in enumerate(beyond(centre)):
        blocks_ref[n * orb : (n + 1) * orb, :] = masked(
            mask_ref, dens_ref, cols // orb - centre + l, s - l + 2 * centre
        )
    half = out_ref.shape[0]
    out_ref[...] = blocks_ref[pl.ds(pl.multiple_of(core * half, half), half), :]


def band_kernel(centre, mask_ref, dens_ref, local_ref, back_ref):
    band_count, cols, orb = dens_ref.shape
    blocks = cols // orb
    local_ref[...] = jnp.zeros_like(local_ref)
    back_ref[...] = jnp.zeros_like(back_ref)
    for l in range(blocks):
        for c in range(band_count):
            s = l + c - centre
            if s < 0:
                back_ref[l * orb : (l + 1) * orb, (s + centre) * orb : (s + centre + 1) * orb] = masked(
                    mask_ref, dens_ref, l, c
                )
            elif s < blocks:
                local_ref[l * orb : (l + 1) * orb, s * orb : (s + 1) * orb] = masked(mask_ref, dens_ref, l, c)


def turned(columns, chunk):
    return side_by_side(columns.reshape(chunk, columns.shape[0] // chunk, columns.shape[1]))


def own_kernel(own_ref, local_ref, back_ref, near_ref, behind_ref, open_ref, later_ref, mixed_ref):
    chunk, rows, cols = own_ref.shape
    wide = back_ref.shape[0]
    own = own_ref[...].reshape(chunk * rows, cols)
    near_ref[...] = turned(own[:, :wide], chunk)
    behind_ref[...] = turned(times(own[:, :wide], back_ref[...]).astype(BF16), chunk)
    open_ref[...] = times(own, local_ref[:, :wide])
    mixed_ref[...] = turned(times(own, local_ref[:, wide:]).astype(BF16), chunk)
    later_ref[...] = turned(own[:, wide:], chunk)


def edge_kernel(count, *refs):
    edges = refs[: count - 1]
    local_ref, own_later_ref, mixed_ref, total_ref, later_ref, part_ref = refs[count - 1 :]
    chunk, rows, wide = edges[0].shape
    later = [own_later_ref[...]]
    for d, edge in enumerate(edges):
        columns = edge[...].reshape(chunk * rows, wide)
        part_ref[d] = times(columns, local_ref[local_ref.shape[0] - wide :, :])
        later.append(turned(columns, chunk))
    later = jnp.concatenate(later, axis=0)
    later_ref[...] = later
    total_ref[...] = times_turned(later, mixed_ref[...])


def inner_kernel(count, centre, *refs):
    rests = refs[: count - 1]
    halo_ref, mine_ref, partner_ref, local_ref, back_ref = refs[count - 1 : count + 4]
    own_total_ref, own_near_ref, own_behind_ref, own_open_ref, later_ref, part_ref = refs[count + 4 : count + 10]
    total_ref, near_ref, behind_ref, open_ref, cross_ref, blocks_ref = refs[count + 10 :]
    chunk, rows, wide = halo_ref.shape
    orb = mine_ref.shape[1]
    core = lax.rem(lax.axis_index("ri"), 2)

    half = partner_ref.shape[0]
    blocks_ref[pl.ds(pl.multiple_of(core * half, half), half), :] = mine_ref[...]
    blocks_ref[pl.ds(pl.multiple_of((1 - core) * half, half), half), :] = partner_ref[...]
    cross_ref[...] = jnp.zeros_like(cross_ref)
    for n, (l, s) in enumerate(beyond(centre)):
        cross_ref[l * orb : (l + 1) * orb, s * orb : (s + 1) * orb] = blocks_ref[n * orb : (n + 1) * orb, :]

    halo = halo_ref[...].reshape(chunk * rows, wide)
    first = turned((own_open_ref[...] + times(halo, cross_ref[...])).astype(BF16), chunk)
    near, behind, mixed = [own_near_ref[...]], [own_behind_ref[...]], []
    for d, rest in enumerate(rests):
        columns = rest[...].reshape(chunk * rows, wide)
        near.append(turned(columns, chunk))
        behind.append(turned(times(columns, back_ref[...]).astype(BF16), chunk))
        whole = part_ref[d] + times(columns, local_ref[:wide, :])
        open_ref[d] = whole[:, :wide]
        mixed.append(turned(whole[:, wide:].astype(BF16), chunk))
    near = jnp.concatenate(near, axis=0)
    behind = jnp.concatenate(behind, axis=0)
    near_ref[...] = near.T
    behind_ref[...] = behind.T
    total_ref[:, :rows] = own_total_ref[...] + times_turned(near, first)
    total_ref[:, rows:] = times_turned(later_ref[...], jnp.concatenate(mixed, axis=0))
    total_ref[:rows, :] += times_turned(turned(halo, chunk), behind)


def outer_kernel(count, plan, sizes, *refs):
    halos = refs[: count - 1]
    inner_ref, near_ref, behind_ref, open_ref, cross_ref, keep_ref, give_ref, kx_ref = refs[count - 1 :]
    chunk, rows, wide = halos[0].shape
    core = lax.rem(lax.axis_index("ri"), 2)
    row = lax.axis_index("row")
    col = lax.axis_index("col")
    mixed = []
    for d, halo in enumerate(halos):
        part = open_ref[d] + times(halo[...].reshape(chunk * rows, wide), cross_ref[...])
        mixed.append(side_by_side(part.astype(BF16).reshape(chunk, rows, wide)))
    columns = times(jnp.concatenate(mixed, axis=0), near_ref[...]).T
    lines = times(jnp.concatenate([side_by_side(halo[...]) for halo in halos], axis=0), behind_ref[...])
    for d in range(count):
        at = slice(d * rows, (d + 1) * rows)
        kx_ref[d, :rows] = inner_ref[:rows, at]
        kx_ref[d, rows:] = inner_ref[rows:, at] + lines[:, at]
        if d > 0:
            kx_ref[d] += columns[:, (d - 1) * rows : d * rows]
    out_rows = count * rows // sizes[2]
    per_group = rows // out_rows
    for ref, side in ((give_ref, 1 - core), (keep_ref, core)):
        for k, (zero, one) in enumerate(zip(*plan)):
            dr = jnp.where(side == 0, zero[0], one[0])
            to_col = col ^ jnp.where(side == 0, zero[1], one[1])
            start = ((to_col // per_group) ^ row) * rows + (to_col % per_group) * out_rows
            ref[k] = kx_ref[dr, pl.ds(pl.multiple_of(start, out_rows), out_rows), :]


def kernel(body, outs, in_specs, scratch=()):
    return pl.pallas_call(
        body,
        out_shape=outs,
        in_specs=in_specs,
        out_specs=[VMEM] * len(outs),
        scratch_shapes=scratch,
        compiler_params=PARAMS,
        cost_estimate=pl.CostEstimate(flops=1, bytes_accessed=1, transcendentals=0),
    )


def per_device(sizes, three_centre, density_band, band_mask):
    n_ri, n_row, n_col = sizes
    funcs, rows, cols = three_centre.shape
    band_count, orb = density_band.shape[1:]
    centre = band_count // 2
    wide = centre * orb
    chunk = funcs // n_row
    core = lax.rem(lax.axis_index("ri"), 2)
    plan = owned(n_row, n_col)
    array = jax.ShapeDtypeStruct
    sems = pltpu.SemaphoreType.DMA

    def forward(i, j, k):
        return i, j, (k + 1) % n_col

    density = jnp.transpose(density_band, (1, 0, 2))
    cuts = kernel(
        functools.partial(cut_kernel, n_row),
        [array((chunk, rows, wide), BF16)] * n_row
        + [array((chunk, rows, cols), BF16)]
        + [array((chunk, rows, cols - wide), BF16)] * (n_row - 1),
        [HBM],
        [sems((2 * n_row,))],
    )(three_centre)
    halo, edges, mine, rests = cuts[0], cuts[1:n_row], cuts[n_row], cuts[n_row + 1 :]
    halo = move(halo, sizes, forward)
    edges = [move(edges[d - 1], sizes, lambda i, j, k, d=d: (i, j ^ d, k)) for d in range(1, n_row)]
    half = len(beyond(centre)) * orb // 2
    (blocks,) = kernel(
        functools.partial(blocks_kernel, centre),
        [array((half, orb), BF16)],
        [VMEM, VMEM],
        [pltpu.VMEM((2 * half, orb), BF16)],
    )(band_mask, density)
    blocks = move(blocks, sizes, forward)
    partner = move(blocks, sizes, lambda i, j, k: (i ^ 1, j, k))
    local, back = kernel(
        functools.partial(band_kernel, centre),
        [array((cols, cols), BF16), array((wide, wide), BF16)],
        [VMEM, VMEM],
    )(band_mask, after(density, blocks))
    whole = n_row * rows
    side = chunk * wide
    *own, own_later, mixed = kernel(
        own_kernel,
        [
            array((rows, side), BF16),
            array((rows, side), BF16),
            array((chunk * rows, wide), F32),
            array((rows, chunk * (cols - wide)), BF16),
            array((rows, chunk * (cols - wide)), BF16),
        ],
        [VMEM] * 3,
    )(mine, local, back)
    halos = [move(after(part, blocks), sizes, forward) for part in edges]
    rests = [
        move(after(rests[d - 1], mixed), sizes, lambda i, j, k, d=d: (i, j ^ d, k))
        for d in range(1, n_row)
    ]

    total, later, part = kernel(
        functools.partial(edge_kernel, n_row),
        [
            array((whole, rows), F32),
            array((whole, chunk * (cols - wide)), BF16),
            array((n_row - 1, chunk * rows, cols), F32),
        ],
        [VMEM] * (n_row + 2),
    )(*edges, local, own_later, mixed)
    first_terms = [total, *own, later, part]
    handed = kernel(
        functools.partial(inner_kernel, n_row, centre),
        [
            array((whole, whole), F32),
            array((side, whole), BF16),
            array((side, whole), BF16),
            array((n_row - 1, chunk * rows, wide), F32),
            array((wide, wide), BF16),
        ],
        [VMEM] * (n_row + 10),
        [pltpu.VMEM((2 * half, orb), BF16)],
    )(*rests, halo, blocks, partner, local, back, *first_terms)

    half = n_row * n_col // 2
    keep, give = kernel(
        functools.partial(outer_kernel, n_row, plan, sizes),
        [array((half, whole // n_col, rows), F32)] * 2,
        [VMEM] * (n_row - 1 + 5),
        [pltpu.VMEM((n_row, whole, rows), F32)],
    )(*halos, *handed)

    got = move(give, sizes, lambda i, j, k: (i ^ 1, j, k))
    pieces = keep + got
    total = jnp.where(core == 0, pieces[plan[0].index((0, 0))], 0.0)
    for n, (zero, one) in enumerate(zip(*plan)):
        def target(i, j, k):
            dr, dc = one if i % 2 else zero
            return None if (dr, dc) == (0, 0) else (i, j ^ dr, k ^ dc)

        total = total + move(pieces[n], sizes, target)
    result = total
    for d in range(2, n_ri, 2):
        result = result + move(total, sizes, lambda i, j, k, d=d: (i ^ d, j, k))
    return result + move(result, sizes, lambda i, j, k: (i ^ 1, j, k))


def solution(mesh):
    sizes = tuple(mesh.shape[axis] for axis in AXES)
    placed = (P("ri", "row", "col"), P("col", None, None), P("col", None))
    return jax.shard_map(
        functools.partial(per_device, sizes), mesh=mesh, in_specs=placed, out_specs=P("col", "row"), check_vma=False
    )
```

```python
import functools

import jax
import jax.numpy as jnp
from jax import lax
from jax.experimental import pallas as pl
from jax.experimental.pallas import tpu as pltpu
from jax.sharding import PartitionSpec as P

AXES = ("ri", "row", "col")
F32 = jnp.float32
BF16 = jnp.bfloat16
VMEM = pl.BlockSpec(memory_space=pltpu.VMEM)
HBM = pl.BlockSpec(memory_space=pltpu.HBM)
SMEM = pl.BlockSpec(memory_space=pltpu.SMEM)
PARAMS = pltpu.CompilerParams(vmem_limit_bytes=32 * 1024 * 1024)


def move(value, sizes, target):
    pairs = []
    for i in range(sizes[0]):
        for j in range(sizes[1]):
            for k in range(sizes[2]):
                to = target(i, j, k)
                if to is not None:
                    pairs.append(((i * sizes[1] + j) * sizes[2] + k, (to[0] * sizes[1] + to[1]) * sizes[2] + to[2]))
    return lax.ppermute(value, AXES, pairs)


def after(value, *earlier):
    return lax.optimization_barrier((value,) + earlier)[0]


def owned(rows, cols):
    sides = ([], [])
    for a in range(rows):
        for b in range(cols):
            sides[b if b < 2 else (a + b + 1) % 2].append((a, b))
    plan = []
    for side in sides:
        side = sorted(side, key=lambda at: (at[0] + at[1], at[0]))
        far = min(side, key=lambda at: (-at[0] - at[1], at[0]))
        side.remove(far)
        plan.append([far, *side[1::-1], *side[2:]])
    return plan


def times(a, b):
    return jnp.dot(a, b, preferred_element_type=F32)


def times_turned(a, b):
    return lax.dot_general(a, b, (((1,), (1,)), ((), ())), preferred_element_type=F32)


def masked(mask_ref, dens_ref, l, c):
    orb = dens_ref.shape[2]
    kept = mask_ref[l : l + 1, c : c + 1].astype(F32)
    return (dens_ref[c, l * orb : (l + 1) * orb, :].astype(F32) * kept).astype(BF16)


def beyond(centre):
    return [(l, s) for l in range(centre) for s in range(l + 1)]


def side_by_side(parts):
    return jnp.concatenate([parts[p] for p in range(parts.shape[0])], axis=1)


def cut(tensor_ref, chunk, index, lo, size, out_ref, sem):
    return pltpu.make_async_copy(tensor_ref.at[pl.ds(index * chunk, chunk), :, pl.ds(lo, size)], out_ref, sem)


def cut_kernel(count, tensor_ref, *refs):
    lasts, mine_ref, rests, sems = refs[:count], refs[count], refs[count + 1 : -1], refs[-1]
    chunk, rows, wide = lasts[0].shape
    cols = tensor_ref.shape[2]
    row = lax.axis_index("row")
    copies = [cut(tensor_ref, chunk, row, 0, cols, mine_ref, sems.at[0])]
    for d, out in enumerate(lasts):
        copies.append(cut(tensor_ref, chunk, row ^ d, cols - wide, wide, out, sems.at[1 + d]))
    for d, out in enumerate(rests):
        copies.append(cut(tensor_ref, chunk, row ^ (d + 1), 0, cols - wide, out, sems.at[1 + count + d]))
    for copy in copies:
        copy.start()
    for copy in copies:
        copy.wait()


def blocks_kernel(centre, mask_ref, dens_ref, out_ref, blocks_ref):
    band_count, cols, orb = dens_ref.shape
    core = lax.rem(lax.axis_index("ri"), 2)
    for n, (l, s) in enumerate(beyond(centre)):
        blocks_ref[n * orb : (n + 1) * orb, :] = masked(
            mask_ref, dens_ref, cols // orb - centre + l, s - l + 2 * centre
        )
    half = out_ref.shape[0]
    out_ref[...] = blocks_ref[pl.ds(pl.multiple_of(core * half, half), half), :]


def band_kernel(centre, mask_ref, dens_ref, local_ref, back_ref):
    band_count, cols, orb = dens_ref.shape
    blocks = cols // orb
    local_ref[...] = jnp.zeros_like(local_ref)
    back_ref[...] = jnp.zeros_like(back_ref)
    for l in range(blocks):
        for c in range(band_count):
            s = l + c - centre
            if s < 0:
                back_ref[l * orb : (l + 1) * orb, (s + centre) * orb : (s + centre + 1) * orb] = masked(
                    mask_ref, dens_ref, l, c
                )
            elif s < blocks:
                local_ref[l * orb : (l + 1) * orb, s * orb : (s + 1) * orb] = masked(mask_ref, dens_ref, l, c)


def turned(columns, chunk):
    return side_by_side(columns.reshape(chunk, columns.shape[0] // chunk, columns.shape[1]))


def own_kernel(own_ref, local_ref, back_ref, near_ref, behind_ref, open_ref, later_ref, mixed_ref):
    chunk, rows, cols = own_ref.shape
    wide = back_ref.shape[0]
    own = own_ref[...].reshape(chunk * rows, cols)
    near_ref[...] = turned(own[:, :wide], chunk)
    behind_ref[...] = turned(times(own[:, :wide], back_ref[...]).astype(BF16), chunk)
    open_ref[...] = times(own, local_ref[:, :wide])
    mixed_ref[...] = turned(times(own, local_ref[:, wide:]).astype(BF16), chunk)
    later_ref[...] = turned(own[:, wide:], chunk)


def edge_kernel(count, *refs):
    edges = refs[: count - 1]
    local_ref, own_later_ref, mixed_ref, total_ref, later_ref, part_ref = refs[count - 1 :]
    chunk, rows, wide = edges[0].shape
    later = [own_later_ref[...]]
    for d, edge in enumerate(edges):
        columns = edge[...].reshape(chunk * rows, wide)
        part_ref[d] = times(columns, local_ref[local_ref.shape[0] - wide :, :])
        later.append(turned(columns, chunk))
    later = jnp.concatenate(later, axis=0)
    later_ref[...] = later
    total_ref[...] = times_turned(later, mixed_ref[...])


def inner_kernel(count, centre, *refs):
    rests = refs[: count - 1]
    halo_ref, mine_ref, partner_ref, local_ref, back_ref = refs[count - 1 : count + 4]
    own_total_ref, own_near_ref, own_behind_ref, own_open_ref, later_ref, part_ref = refs[count + 4 : count + 10]
    total_ref, near_ref, behind_ref, open_ref, cross_ref, blocks_ref = refs[count + 10 :]
    chunk, rows, wide = halo_ref.shape
    orb = mine_ref.shape[1]
    core = lax.rem(lax.axis_index("ri"), 2)

    half = partner_ref.shape[0]
    blocks_ref[pl.ds(pl.multiple_of(core * half, half), half), :] = mine_ref[...]
    blocks_ref[pl.ds(pl.multiple_of((1 - core) * half, half), half), :] = partner_ref[...]
    cross_ref[...] = jnp.zeros_like(cross_ref)
    for n, (l, s) in enumerate(beyond(centre)):
        cross_ref[l * orb : (l + 1) * orb, s * orb : (s + 1) * orb] = blocks_ref[n * orb : (n + 1) * orb, :]

    halo = halo_ref[...].reshape(chunk * rows, wide)
    first = turned((own_open_ref[...] + times(halo, cross_ref[...])).astype(BF16), chunk)
    near, behind, mixed = [own_near_ref[...]], [own_behind_ref[...]], []
    for d, rest in enumerate(rests):
        columns = rest[...].reshape(chunk * rows, wide)
        near.append(turned(columns, chunk))
        behind.append(turned(times(columns, back_ref[...]).astype(BF16), chunk))
        whole = part_ref[d] + times(columns, local_ref[:wide, :])
        open_ref[d] = whole[:, :wide]
        mixed.append(turned(whole[:, wide:].astype(BF16), chunk))
    near = jnp.concatenate(near, axis=0)
    behind = jnp.concatenate(behind, axis=0)
    near_ref[...] = near.T
    behind_ref[...] = behind.T
    total_ref[:, :rows] = own_total_ref[...] + times_turned(near, first)
    total_ref[:, rows:] = times_turned(later_ref[...], jnp.concatenate(mixed, axis=0))
    total_ref[:rows, :] += times_turned(turned(halo, chunk), behind)


def outer_kernel(count, plan, sizes, *refs):
    halos = refs[: count - 1]
    inner_ref, near_ref, behind_ref, open_ref, cross_ref, keep_ref, give_ref, kx_ref = refs[count - 1 :]
    chunk, rows, wide = halos[0].shape
    core = lax.rem(lax.axis_index("ri"), 2)
    row = lax.axis_index("row")
    col = lax.axis_index("col")
    mixed = []
    for d, halo in enumerate(halos):
        part = open_ref[d] + times(halo[...].reshape(chunk * rows, wide), cross_ref[...])
        mixed.append(side_by_side(part.astype(BF16).reshape(chunk, rows, wide)))
    columns = times(jnp.concatenate(mixed, axis=0), near_ref[...]).T
    lines = times(jnp.concatenate([side_by_side(halo[...]) for halo in halos], axis=0), behind_ref[...])
    for d in range(count):
        at = slice(d * rows, (d + 1) * rows)
        kx_ref[d, :rows] = inner_ref[:rows, at]
        kx_ref[d, rows:] = inner_ref[rows:, at] + lines[:, at]
        if d > 0:
            kx_ref[d] += columns[:, (d - 1) * rows : d * rows]
    out_rows = count * rows // sizes[2]
    per_group = rows // out_rows
    for ref, side in ((give_ref, 1 - core), (keep_ref, core)):
        for k, (zero, one) in enumerate(zip(*plan)):
            dr = jnp.where(side == 0, zero[0], one[0])
            to_col = col ^ jnp.where(side == 0, zero[1], one[1])
            start = ((to_col // per_group) ^ row) * rows + (to_col % per_group) * out_rows
            ref[k] = kx_ref[dr, pl.ds(pl.multiple_of(start, out_rows), out_rows), :]


def kernel(body, outs, in_specs, scratch=()):
    return pl.pallas_call(
        body,
        out_shape=outs,
        in_specs=in_specs,
        out_specs=[VMEM] * len(outs),
        scratch_shapes=scratch,
        compiler_params=PARAMS,
        cost_estimate=pl.CostEstimate(flops=1, bytes_accessed=1, transcendentals=0),
    )


def per_device(sizes, three_centre, density_band, band_mask):
    n_ri, n_row, n_col = sizes
    funcs, rows, cols = three_centre.shape
    band_count, orb = density_band.shape[1:]
    centre = band_count // 2
    wide = centre * orb
    chunk = funcs // n_row
    core = lax.rem(lax.axis_index("ri"), 2)
    plan = owned(n_row, n_col)
    array = jax.ShapeDtypeStruct
    sems = pltpu.SemaphoreType.DMA

    def forward(i, j, k):
        return i, j, (k + 1) % n_col

    density = jnp.transpose(density_band, (1, 0, 2))
    cuts = kernel(
        functools.partial(cut_kernel, n_row),
        [array((chunk, rows, wide), BF16)] * n_row
        + [array((chunk, rows, cols), BF16)]
        + [array((chunk, rows, cols - wide), BF16)] * (n_row - 1),
        [HBM],
        [sems((2 * n_row,))],
    )(three_centre)
    halo, edges, mine, rests = cuts[0], cuts[1:n_row], cuts[n_row], cuts[n_row + 1 :]
    halo = move(halo, sizes, forward)
    edges = [move(edges[d - 1], sizes, lambda i, j, k, d=d: (i, j ^ d, k)) for d in range(1, n_row)]
    half = len(beyond(centre)) * orb // 2
    (blocks,) = kernel(
        functools.partial(blocks_kernel, centre),
        [array((half, orb), BF16)],
        [VMEM, VMEM],
        [pltpu.VMEM((2 * half, orb), BF16)],
    )(band_mask, density)
    blocks = move(blocks, sizes, forward)
    partner = move(blocks, sizes, lambda i, j, k: (i ^ 1, j, k))
    local, back = kernel(
        functools.partial(band_kernel, centre),
        [array((cols, cols), BF16), array((wide, wide), BF16)],
        [VMEM, VMEM],
    )(band_mask, after(density, blocks))
    whole = n_row * rows
    side = chunk * wide
    *own, own_later, mixed = kernel(
        own_kernel,
        [
            array((rows, side), BF16),
            array((rows, side), BF16),
            array((chunk * rows, wide), F32),
            array((rows, chunk * (cols - wide)), BF16),
            array((rows, chunk * (cols - wide)), BF16),
        ],
        [VMEM] * 3,
    )(mine, local, back)
    halos = [move(after(part, blocks), sizes, forward) for part in edges]
    rests = [
        move(after(rests[d - 1], blocks), sizes, lambda i, j, k, d=d: (i, j ^ d, k))
        for d in range(1, n_row)
    ]

    total, later, part = kernel(
        functools.partial(edge_kernel, n_row),
        [
            array((whole, rows), F32),
            array((whole, chunk * (cols - wide)), BF16),
            array((n_row - 1, chunk * rows, cols), F32),
        ],
        [VMEM] * (n_row + 2),
    )(*edges, local, own_later, mixed)
    first_terms = [total, *own, later, part]
    handed = kernel(
        functools.partial(inner_kernel, n_row, centre),
        [
            array((whole, whole), F32),
            array((side, whole), BF16),
            array((side, whole), BF16),
            array((n_row - 1, chunk * rows, wide), F32),
            array((wide, wide), BF16),
        ],
        [VMEM] * (n_row + 10),
        [pltpu.VMEM((2 * half, orb), BF16)],
    )(*rests, halo, blocks, partner, local, back, *first_terms)

    half = n_row * n_col // 2
    keep, give = kernel(
        functools.partial(outer_kernel, n_row, plan, sizes),
        [array((half, whole // n_col, rows), F32)] * 2,
        [VMEM] * (n_row - 1 + 5),
        [pltpu.VMEM((n_row, whole, rows), F32)],
    )(*halos, *handed)

    got = move(give, sizes, lambda i, j, k: (i ^ 1, j, k))
    pieces = keep + got
    total = jnp.where(core == 0, pieces[plan[0].index((0, 0))], 0.0)
    for n, (zero, one) in enumerate(zip(*plan)):
        def target(i, j, k):
            dr, dc = one if i % 2 else zero
            return None if (dr, dc) == (0, 0) else (i, j ^ dr, k ^ dc)

        total = total + move(pieces[n], sizes, target)
    result = total
    for d in range(2, n_ri, 2):
        result = result + move(total, sizes, lambda i, j, k, d=d: (i ^ d, j, k))
    return result + move(result, sizes, lambda i, j, k: (i ^ 1, j, k))


def solution(mesh):
    sizes = tuple(mesh.shape[axis] for axis in AXES)
    placed = (P("ri", "row", "col"), P("col", None, None), P("col", None))
    return jax.shard_map(
        functools.partial(per_device, sizes), mesh=mesh, in_specs=placed, out_specs=P("col", "row"), check_vma=False
    )
```

```python
import functools

import jax
import jax.numpy as jnp
from jax import lax
from jax.experimental import pallas as pl
from jax.experimental.pallas import tpu as pltpu
from jax.sharding import PartitionSpec as P

AXES = ("ri", "row", "col")
F32 = jnp.float32
BF16 = jnp.bfloat16
VMEM = pl.BlockSpec(memory_space=pltpu.VMEM)
HBM = pl.BlockSpec(memory_space=pltpu.HBM)
SMEM = pl.BlockSpec(memory_space=pltpu.SMEM)
PARAMS = pltpu.CompilerParams(vmem_limit_bytes=32 * 1024 * 1024)


def move(value, sizes, target):
    pairs = []
    for i in range(sizes[0]):
        for j in range(sizes[1]):
            for k in range(sizes[2]):
                to = target(i, j, k)
                if to is not None:
                    pairs.append(((i * sizes[1] + j) * sizes[2] + k, (to[0] * sizes[1] + to[1]) * sizes[2] + to[2]))
    return lax.ppermute(value, AXES, pairs)


def after(value, *earlier):
    return lax.optimization_barrier((value,) + earlier)[0]


def owned(rows, cols):
    sides = ([], [])
    for a in range(rows):
        for b in range(cols):
            sides[b if b < 2 else (a + b + 1) % 2].append((a, b))
    plan = []
    for side in sides:
        side = sorted(side, key=lambda at: (at[0] + at[1], at[0]))
        far = min(side, key=lambda at: (-at[0] - at[1], at[0]))
        side.remove(far)
        plan.append([far, *side[1::-1], *side[2:]])
    return plan


def times(a, b):
    return jnp.dot(a, b, preferred_element_type=F32)


def times_turned(a, b):
    return lax.dot_general(a, b, (((1,), (1,)), ((), ())), preferred_element_type=F32)


def masked(mask_ref, dens_ref, l, c):
    orb = dens_ref.shape[2]
    kept = mask_ref[l : l + 1, c : c + 1].astype(F32)
    return (dens_ref[c, l * orb : (l + 1) * orb, :].astype(F32) * kept).astype(BF16)


def beyond(centre):
    return [(l, s) for l in range(centre) for s in range(l + 1)]


def side_by_side(parts):
    return jnp.concatenate([parts[p] for p in range(parts.shape[0])], axis=1)


def cut(tensor_ref, chunk, index, lo, size, out_ref, sem):
    return pltpu.make_async_copy(tensor_ref.at[pl.ds(index * chunk, chunk), :, pl.ds(lo, size)], out_ref, sem)


def cut_kernel(count, tensor_ref, *refs):
    lasts, mine_ref, rests, sems = refs[:count], refs[count], refs[count + 1 : -1], refs[-1]
    chunk, rows, wide = lasts[0].shape
    cols = tensor_ref.shape[2]
    row = lax.axis_index("row")
    copies = [cut(tensor_ref, chunk, row, 0, cols, mine_ref, sems.at[0])]
    for d, out in enumerate(lasts):
        copies.append(cut(tensor_ref, chunk, row ^ d, cols - wide, wide, out, sems.at[1 + d]))
    for d, out in enumerate(rests):
        copies.append(cut(tensor_ref, chunk, row ^ (d + 1), 0, cols - wide, out, sems.at[1 + count + d]))
    for copy in copies:
        copy.start()
    for copy in copies:
        copy.wait()


def blocks_kernel(centre, mask_ref, dens_ref, out_ref, blocks_ref):
    band_count, cols, orb = dens_ref.shape
    core = lax.rem(lax.axis_index("ri"), 2)
    for n, (l, s) in enumerate(beyond(centre)):
        blocks_ref[n * orb : (n + 1) * orb, :] = masked(
            mask_ref, dens_ref, cols // orb - centre + l, s - l + 2 * centre
        )
    half = out_ref.shape[0]
    out_ref[...] = blocks_ref[pl.ds(pl.multiple_of(core * half, half), half), :]


def band_kernel(centre, mask_ref, dens_ref, local_ref, back_ref):
    band_count, cols, orb = dens_ref.shape
    blocks = cols // orb
    local_ref[...] = jnp.zeros_like(local_ref)
    back_ref[...] = jnp.zeros_like(back_ref)
    for l in range(blocks):
        for c in range(band_count):
            s = l + c - centre
            if s < 0:
                back_ref[l * orb : (l + 1) * orb, (s + centre) * orb : (s + centre + 1) * orb] = masked(
                    mask_ref, dens_ref, l, c
                )
            elif s < blocks:
                local_ref[l * orb : (l + 1) * orb, s * orb : (s + 1) * orb] = masked(mask_ref, dens_ref, l, c)


def turned(columns, chunk):
    return side_by_side(columns.reshape(chunk, columns.shape[0] // chunk, columns.shape[1]))


def own_kernel(own_ref, local_ref, back_ref, near_ref, behind_ref, open_ref, later_ref, mixed_ref):
    chunk, rows, cols = own_ref.shape
    wide = back_ref.shape[0]
    own = own_ref[...].reshape(chunk * rows, cols)
    near_ref[...] = turned(own[:, :wide], chunk)
    behind_ref[...] = turned(times(own[:, :wide], back_ref[...]).astype(BF16), chunk)
    open_ref[...] = times(own, local_ref[:, :wide])
    mixed_ref[...] = turned(times(own, local_ref[:, wide:]).astype(BF16), chunk)
    later_ref[...] = turned(own[:, wide:], chunk)


def edge_kernel(count, *refs):
    edges = refs[: count - 1]
    local_ref, own_later_ref, mixed_ref, total_ref, later_ref, part_ref = refs[count - 1 :]
    chunk, rows, wide = edges[0].shape
    later = [own_later_ref[...]]
    for d, edge in enumerate(edges):
        columns = edge[...].reshape(chunk * rows, wide)
        part_ref[d] = times(columns, local_ref[local_ref.shape[0] - wide :, :])
        later.append(turned(columns, chunk))
    later = jnp.concatenate(later, axis=0)
    later_ref[...] = later
    total_ref[...] = times_turned(later, mixed_ref[...])


def inner_kernel(count, centre, *refs):
    rests = refs[: count - 1]
    halo_ref, mine_ref, partner_ref, local_ref, back_ref = refs[count - 1 : count + 4]
    own_total_ref, own_near_ref, own_behind_ref, own_open_ref, later_ref, part_ref = refs[count + 4 : count + 10]
    total_ref, near_ref, behind_ref, open_ref, cross_ref, blocks_ref = refs[count + 10 :]
    chunk, rows, wide = halo_ref.shape
    orb = mine_ref.shape[1]
    core = lax.rem(lax.axis_index("ri"), 2)

    half = partner_ref.shape[0]
    blocks_ref[pl.ds(pl.multiple_of(core * half, half), half), :] = mine_ref[...]
    blocks_ref[pl.ds(pl.multiple_of((1 - core) * half, half), half), :] = partner_ref[...]
    cross_ref[...] = jnp.zeros_like(cross_ref)
    for n, (l, s) in enumerate(beyond(centre)):
        cross_ref[l * orb : (l + 1) * orb, s * orb : (s + 1) * orb] = blocks_ref[n * orb : (n + 1) * orb, :]

    halo = halo_ref[...].reshape(chunk * rows, wide)
    first = turned((own_open_ref[...] + times(halo, cross_ref[...])).astype(BF16), chunk)
    near, behind, mixed = [own_near_ref[...]], [own_behind_ref[...]], []
    for d, rest in enumerate(rests):
        columns = rest[...].reshape(chunk * rows, wide)
        near.append(turned(columns, chunk))
        behind.append(turned(times(columns, back_ref[...]).astype(BF16), chunk))
        whole = part_ref[d] + times(columns, local_ref[:wide, :])
        open_ref[d] = whole[:, :wide]
        mixed.append(turned(whole[:, wide:].astype(BF16), chunk))
    near = jnp.concatenate(near, axis=0)
    behind = jnp.concatenate(behind, axis=0)
    near_ref[...] = near.T
    behind_ref[...] = behind.T
    total_ref[:, :rows] = own_total_ref[...] + times_turned(near, first)
    total_ref[:, rows:] = times_turned(later_ref[...], jnp.concatenate(mixed, axis=0))
    total_ref[:rows, :] += times_turned(turned(halo, chunk), behind)


def outer_kernel(count, plan, sizes, *refs):
    halos = refs[: count - 1]
    inner_ref, near_ref, behind_ref, open_ref, cross_ref, keep_ref, give_ref, kx_ref = refs[count - 1 :]
    chunk, rows, wide = halos[0].shape
    core = lax.rem(lax.axis_index("ri"), 2)
    row = lax.axis_index("row")
    col = lax.axis_index("col")
    mixed = []
    for d, halo in enumerate(halos):
        part = open_ref[d] + times(halo[...].reshape(chunk * rows, wide), cross_ref[...])
        mixed.append(side_by_side(part.astype(BF16).reshape(chunk, rows, wide)))
    columns = times(jnp.concatenate(mixed, axis=0), near_ref[...]).T
    lines = times(jnp.concatenate([side_by_side(halo[...]) for halo in halos], axis=0), behind_ref[...])
    for d in range(count):
        at = slice(d * rows, (d + 1) * rows)
        upper, lower = inner_ref[:rows, at], inner_ref[rows:, at] + lines[:, at]
        if d > 0:
            add = columns[:, (d - 1) * rows : d * rows]
            upper, lower = upper + add[:rows], lower + add[rows:]
        kx_ref[d, :rows] = upper
        kx_ref[d, rows:] = lower
    out_rows = count * rows // sizes[2]
    per_group = rows // out_rows
    for ref, side in ((give_ref, 1 - core), (keep_ref, core)):
        for k, (zero, one) in enumerate(zip(*plan)):
            dr = jnp.where(side == 0, zero[0], one[0])
            to_col = col ^ jnp.where(side == 0, zero[1], one[1])
            start = ((to_col // per_group) ^ row) * rows + (to_col % per_group) * out_rows
            ref[k] = kx_ref[dr, pl.ds(pl.multiple_of(start, out_rows), out_rows), :]


def kernel(body, outs, in_specs, scratch=()):
    return pl.pallas_call(
        body,
        out_shape=outs,
        in_specs=in_specs,
        out_specs=[VMEM] * len(outs),
        scratch_shapes=scratch,
        compiler_params=PARAMS,
        cost_estimate=pl.CostEstimate(flops=1, bytes_accessed=1, transcendentals=0),
    )


def per_device(sizes, three_centre, density_band, band_mask):
    n_ri, n_row, n_col = sizes
    funcs, rows, cols = three_centre.shape
    band_count, orb = density_band.shape[1:]
    centre = band_count // 2
    wide = centre * orb
    chunk = funcs // n_row
    core = lax.rem(lax.axis_index("ri"), 2)
    plan = owned(n_row, n_col)
    array = jax.ShapeDtypeStruct
    sems = pltpu.SemaphoreType.DMA

    def forward(i, j, k):
        return i, j, (k + 1) % n_col

    density = jnp.transpose(density_band, (1, 0, 2))
    cuts = kernel(
        functools.partial(cut_kernel, n_row),
        [array((chunk, rows, wide), BF16)] * n_row
        + [array((chunk, rows, cols), BF16)]
        + [array((chunk, rows, cols - wide), BF16)] * (n_row - 1),
        [HBM],
        [sems((2 * n_row,))],
    )(three_centre)
    halo, edges, mine, rests = cuts[0], cuts[1:n_row], cuts[n_row], cuts[n_row + 1 :]
    halo = move(halo, sizes, forward)
    edges = [move(edges[d - 1], sizes, lambda i, j, k, d=d: (i, j ^ d, k)) for d in range(1, n_row)]
    half = len(beyond(centre)) * orb // 2
    (blocks,) = kernel(
        functools.partial(blocks_kernel, centre),
        [array((half, orb), BF16)],
        [VMEM, VMEM],
        [pltpu.VMEM((2 * half, orb), BF16)],
    )(band_mask, density)
    blocks = move(blocks, sizes, forward)
    partner = move(blocks, sizes, lambda i, j, k: (i ^ 1, j, k))
    local, back = kernel(
        functools.partial(band_kernel, centre),
        [array((cols, cols), BF16), array((wide, wide), BF16)],
        [VMEM, VMEM],
    )(band_mask, after(density, blocks))
    whole = n_row * rows
    side = chunk * wide
    *own, own_later, mixed = kernel(
        own_kernel,
        [
            array((rows, side), BF16),
            array((rows, side), BF16),
            array((chunk * rows, wide), F32),
            array((rows, chunk * (cols - wide)), BF16),
            array((rows, chunk * (cols - wide)), BF16),
        ],
        [VMEM] * 3,
    )(mine, local, back)
    halos = [move(after(part, blocks), sizes, forward) for part in edges]
    rests = [
        move(after(rests[d - 1], blocks), sizes, lambda i, j, k, d=d: (i, j ^ d, k))
        for d in range(1, n_row)
    ]

    total, later, part = kernel(
        functools.partial(edge_kernel, n_row),
        [
            array((whole, rows), F32),
            array((whole, chunk * (cols - wide)), BF16),
            array((n_row - 1, chunk * rows, cols), F32),
        ],
        [VMEM] * (n_row + 2),
    )(*edges, local, own_later, mixed)
    first_terms = [total, *own, later, part]
    handed = kernel(
        functools.partial(inner_kernel, n_row, centre),
        [
            array((whole, whole), F32),
            array((side, whole), BF16),
            array((side, whole), BF16),
            array((n_row - 1, chunk * rows, wide), F32),
            array((wide, wide), BF16),
        ],
        [VMEM] * (n_row + 10),
        [pltpu.VMEM((2 * half, orb), BF16)],
    )(*rests, halo, blocks, partner, local, back, *first_terms)

    half = n_row * n_col // 2
    keep, give = kernel(
        functools.partial(outer_kernel, n_row, plan, sizes),
        [array((half, whole // n_col, rows), F32)] * 2,
        [VMEM] * (n_row - 1 + 5),
        [pltpu.VMEM((n_row, whole, rows), F32)],
    )(*halos, *handed)

    got = move(give, sizes, lambda i, j, k: (i ^ 1, j, k))
    pieces = keep + got
    total = jnp.where(core == 0, pieces[plan[0].index((0, 0))], 0.0)
    for n, (zero, one) in enumerate(zip(*plan)):
        def target(i, j, k):
            dr, dc = one if i % 2 else zero
            return None if (dr, dc) == (0, 0) else (i, j ^ dr, k ^ dc)

        total = total + move(pieces[n], sizes, target)
    result = total
    for d in range(2, n_ri, 2):
        result = result + move(total, sizes, lambda i, j, k, d=d: (i ^ d, j, k))
    return result + move(result, sizes, lambda i, j, k: (i ^ 1, j, k))


def solution(mesh):
    sizes = tuple(mesh.shape[axis] for axis in AXES)
    placed = (P("ri", "row", "col"), P("col", None, None), P("col", None))
    return jax.shard_map(
        functools.partial(per_device, sizes), mesh=mesh, in_specs=placed, out_specs=P("col", "row"), check_vma=False
    )
```
